32 devices in a mesh: ctx: 4 (over z), fsdp: 8 (over y, x, core).
Axes of the slice: x: 2, y: 2, z: 4, core: 2. Of those that a mesh axis runs over, the one named last changes fastest.
Arguments:
- queries: bfloat16 [8, 1024, 2048], P('fsdp', 'ctx'), may hold values from -36 to 36
- keys: bfloat16 [8, 1024, 512], P('fsdp', 'ctx'), may hold values from -6 to 6
- values: bfloat16 [8, 1024, 512], P('fsdp', 'ctx'), may hold values from -6 to 6
- resid: bfloat16 [8, 1024, 2048], P('fsdp', 'ctx'), may hold values from -6 to 6
- grad_out: bfloat16 [8, 1024, 2048], P('fsdp', 'ctx'), may hold values from -8 to 8
- w_out: bfloat16 [2048, 2048], P(None, 'fsdp'), may hold values from -0.125 to 0.125
- block_list: int32 [8, 8], P('ctx'), may hold values from 0 to 7, as said below
- block_count: int32 [8], P('ctx'), may hold values from 1 to 8, as said below
Outputs:
- mixed: bfloat16 [8, 1024, 2048], P('fsdp', 'ctx')
- query_grad: bfloat16 [8, 1024, 2048], P('fsdp', 'ctx')
- key_grad: bfloat16 [8, 1024, 512], P('fsdp', 'ctx')
- value_grad: bfloat16 [8, 1024, 512], P('fsdp', 'ctx')
- proj_grad: float32 [2048, 2048], P('ctx', 'fsdp')
The draws below stay inside these ranges and needn't reach their ends.
Inputs may be any that keep to these rules, and one draw needn't show every extreme that they name: `block_list`: row r lists the key blocks of query block r within its sequence: entry 0 is r itself; entries 1 to block_count[r] - 1 are distinct blocks before r; entries from block_count[r] on are ignored and hold r or earlier blocks. block_count[r] is at most min(r + 1, 8); the last query block has exactly 8.
All inputs are finite; a program needn't handle non-finite values.
Results may differ from the reference program's by a relative error of at most 0.025.
Values may be sent and summed in bfloat16 or wider, within the bound.
No kernel may reach another device: no remote copies, remote signals or barrier semaphores. Data moves between devices by JAX's collectives and lax.ppermute only.
A program may use at most 192 MiB of HBM per device.

```python
import math
import jax
import jax.numpy as jnp
from jax import lax

D = 2048
QUERY_HEADS = 16
KEY_VALUE_HEADS = 4
HEAD_DIM = 128
BLOCK_SIZE = 128
KEY_SLOTS = 8
SEQ_LENGTH = 1024
BLOCKS_PER_SEQ = 8
SEQUENCE_COUNT = 8
N_CTX = 4


def query_key_pair(key):
    base = jax.random.fold_in(key, 7)
    query_key, key_random_seed = jax.random.split(base, 2)
    query_sample = jnp.clip(jax.random.normal(query_key, (SEQUENCE_COUNT, SEQ_LENGTH, QUERY_HEADS, HEAD_DIM), jnp.float32), -6.0, 6.0)
    key_sample = jnp.clip(jax.random.normal(key_random_seed, (SEQUENCE_COUNT, SEQ_LENGTH, KEY_VALUE_HEADS, HEAD_DIM), jnp.float32), -6.0, 6.0)
    return (query_sample.reshape(SEQUENCE_COUNT, SEQ_LENGTH, QUERY_HEADS * HEAD_DIM), key_sample.reshape(SEQUENCE_COUNT, SEQ_LENGTH, KEY_VALUE_HEADS * HEAD_DIM))


def draw_queries(key, part):
    return query_key_pair(key)[0].astype(jnp.bfloat16)


def draw_keys(key, part):
    return query_key_pair(key)[1].astype(jnp.bfloat16)


def block_pattern(key):
    base = jax.random.fold_in(key, 11)
    count_key, order_key = jax.random.split(base)
    block_ids = jnp.arange(BLOCKS_PER_SEQ, dtype=jnp.int32)
    limit = jnp.minimum(block_ids + 1, KEY_SLOTS)
    counts = jax.random.randint(count_key, (BLOCKS_PER_SEQ,), 0, 1 << 20, jnp.int32) % limit + 1
    counts = jnp.where(block_ids == BLOCKS_PER_SEQ - 1, KEY_SLOTS, counts).astype(jnp.int32)
    ranks = jax.random.randint(order_key, (BLOCKS_PER_SEQ, BLOCKS_PER_SEQ), 0, 1 << 16, jnp.int32) * BLOCKS_PER_SEQ + block_ids[None, :]
    earlier = block_ids[None, :] < block_ids[:, None]
    ranks = jnp.where(earlier, ranks, -1 - block_ids[None, :])
    ordered = jnp.argsort(-ranks, axis=1, stable=True).astype(jnp.int32)
    chosen = ordered[:, :KEY_SLOTS - 1]
    usable = jnp.arange(KEY_SLOTS - 1, dtype=jnp.int32)[None, :] < block_ids[:, None]
    chosen = jnp.where(usable, chosen, block_ids[:, None])
    listing = jnp.concatenate([block_ids[:, None], chosen], axis=1).astype(jnp.int32)
    return (listing, counts)


def draw_block_list(key, part):
    return block_pattern(key)[0]


def draw_block_count(key, part):
    return block_pattern(key)[1]


def with_spikes(result, stream_key, source, target, blocks, factor):
    owner, partner = [(jnp.arange(result.shape[axis_at]) // (result.shape[axis_at] // blocks)).reshape([-1 if axis == axis_at else 1 for axis in range(result.ndim)]) for axis_at in (source, target)]
    chosen = jax.random.permutation(stream_key, blocks)[partner]
    strong = (owner == chosen) | (owner == (partner + blocks // 2) % blocks)
    return jnp.where(strong, factor * result, result)


def level_of(stream_key, dims, cuts, low, largest):
    def one(dim, parts):
        heights = jax.random.uniform(jax.random.fold_in(jax.random.fold_in(stream_key, 6), dim), (parts,), jnp.float32, low / len(cuts), largest / len(cuts))
        return jnp.repeat(jnp.exp(heights), dims[dim] // parts).reshape((-1,) + (1,) * (len(dims) - dim - 1))

    level = one(*cuts[0])
    for cut in cuts[1:]:
        level = level * one(*cut)
    return level


def scatter_about(key, shape, spread, reach, pieces=(), held_as=jnp.bfloat16):
    values = spread * jax.random.normal(key, shape, jnp.float32)
    if pieces:
        values = values * level_of(key, shape, pieces, -0.22, 0.18)
    return jnp.clip(values, -reach, reach).astype(held_as)


def heavy_noise(stream_key, dims, spread, reach, cuts, heavy, kind=jnp.bfloat16):
    array = spread * jax.random.normal(stream_key, dims, jnp.float32)
    if cuts:
        array = array * level_of(stream_key, dims, cuts, -0.22, 0.18)
    return jnp.clip(with_spikes(array, jax.random.fold_in(stream_key, 3), *heavy), -reach, reach).astype(kind)


def setup_inputs(seed: int = 0) -> dict:
    key_list = jax.random.split(jax.random.key(seed), 9)
    queries = draw_queries(jax.random.fold_in(key_list[8], 71), 0)
    keys = draw_keys(jax.random.fold_in(key_list[8], 71), 0)
    values = scatter_about(key_list[2], (SEQUENCE_COUNT, SEQ_LENGTH, KEY_VALUE_HEADS * HEAD_DIM), 1.0, 6.0, ((0, 8), (1, 4)))
    resid = scatter_about(key_list[3], (SEQUENCE_COUNT, SEQ_LENGTH, D), 1.0, 6.0, ((0, 8), (1, 4)))
    grad_out = heavy_noise(key_list[4], (SEQUENCE_COUNT, SEQ_LENGTH, D), 1.0, 8.0, ((0, 8), (1, 4)), (0, 2, 8, 2.0))
    w_out = scatter_about(key_list[5], (QUERY_HEADS * HEAD_DIM, D), (QUERY_HEADS * HEAD_DIM) ** -0.5, 0.125, ((1, 8),))
    block_list = draw_block_list(jax.random.fold_in(key_list[8], 71), 0)
    block_count = draw_block_count(jax.random.fold_in(key_list[8], 71), 0)
    return dict(queries=queries, keys=keys, values=values, resid=resid, grad_out=grad_out, w_out=w_out, block_list=block_list, block_count=block_count)


def score_mask(first_row, listed_blocks, live_count):
    query_pos = first_row + jnp.arange(BLOCK_SIZE, dtype=jnp.int32)
    key_pos = listed_blocks[:, None] * BLOCK_SIZE + jnp.arange(BLOCK_SIZE, dtype=jnp.int32)[None, :]
    slot_live = jnp.arange(KEY_SLOTS, dtype=jnp.int32) < live_count
    return (key_pos[None, :, :] <= query_pos[:, None, None]) & slot_live[None, :, None]

def block_weights(query_blk, key_sel, allowed):
    scale = 1.0 / math.sqrt(HEAD_DIM)
    scores = jnp.einsum('qgrd,sbgd->grqsb', query_blk.astype(jnp.float32), key_sel.astype(jnp.float32)) * scale
    scores = jnp.where(allowed[None, None], scores, jnp.float32(-1e+30))
    top = lax.optimization_barrier(jnp.max(scores, axis=(3, 4), keepdims=True))
    expon = jnp.exp(scores - top)
    probs = expon / lax.optimization_barrier(jnp.sum(expon, axis=(3, 4), keepdims=True))
    return (probs, probs.astype(jnp.bfloat16))

def reference(queries, keys, values, resid, grad_out, w_out, block_list, block_count):
    scale = 1.0 / math.sqrt(HEAD_DIM)
    query_groups = QUERY_HEADS // KEY_VALUE_HEADS
    positions = jnp.arange(BLOCKS_PER_SEQ, dtype=jnp.int32)

    def one_sequence(operands):
        query_sequence, key_sequence, value_sequence, resid_seq, grad_seq = operands
        blocked_keys = key_sequence.reshape(BLOCKS_PER_SEQ, BLOCK_SIZE, KEY_VALUE_HEADS, HEAD_DIM)
        blocked_values = value_sequence.reshape(BLOCKS_PER_SEQ, BLOCK_SIZE, KEY_VALUE_HEADS, HEAD_DIM)
        blocked_queries = query_sequence.reshape(BLOCKS_PER_SEQ, BLOCK_SIZE, KEY_VALUE_HEADS, query_groups, HEAD_DIM)

        def forward_block(block_pos):
            listed_blocks = block_list[block_pos]
            allowed = score_mask(block_pos * BLOCK_SIZE, listed_blocks, block_count[block_pos])
            key_sel = jnp.take(blocked_keys, listed_blocks, axis=0)
            value_sel = jnp.take(blocked_values, listed_blocks, axis=0)
            probs, probs_b = block_weights(blocked_queries[block_pos], key_sel, allowed)
            attended = jnp.einsum('grqsb,sbgd->qgrd', probs_b.astype(jnp.float32), value_sel.astype(jnp.float32))
            return attended.astype(jnp.bfloat16)
        out_blocks = lax.map(forward_block, positions)
        out_rows = out_blocks.reshape(SEQ_LENGTH, QUERY_HEADS * HEAD_DIM)
        mixed = (resid_seq.astype(jnp.float32) + jnp.dot(out_rows, w_out, preferred_element_type=jnp.float32)).astype(jnp.bfloat16)
        attended_gradient = lax.dot_general(grad_seq, w_out, (((1,), (1,)), ((), ())), preferred_element_type=jnp.float32).astype(jnp.bfloat16)
        output_grad_blocks = attended_gradient.reshape(BLOCKS_PER_SEQ, BLOCK_SIZE, KEY_VALUE_HEADS, query_groups, HEAD_DIM)

        def backward_block(block_pos):
            listed_blocks = block_list[block_pos]
            allowed = score_mask(block_pos * BLOCK_SIZE, listed_blocks, block_count[block_pos])
            key_sel = jnp.take(blocked_keys, listed_blocks, axis=0)
            value_sel = jnp.take(blocked_values, listed_blocks, axis=0)
            query_blk = blocked_queries[block_pos]
            dout_blk = output_grad_blocks[block_pos]
            probs, probs_b = block_weights(query_blk, key_sel, allowed)
            value_part = jnp.einsum('grqsb,qgrd->sbgd', probs_b.astype(jnp.float32), dout_blk.astype(jnp.float32))
            prob_grads = jnp.einsum('qgrd,sbgd->grqsb', dout_blk.astype(jnp.float32), value_sel.astype(jnp.float32))
            row_dot = lax.optimization_barrier(jnp.sum(dout_blk.astype(jnp.float32) * out_blocks[block_pos].astype(jnp.float32), axis=-1))
            row_dot = jnp.transpose(row_dot, (1, 2, 0))[:, :, :, None, None]
            score_grads = (probs * (prob_grads - row_dot) * scale).astype(jnp.bfloat16)
            query_part = jnp.einsum('grqsb,sbgd->qgrd', score_grads.astype(jnp.float32), key_sel.astype(jnp.float32)).astype(jnp.bfloat16)
            key_part = jnp.einsum('grqsb,qgrd->sbgd', score_grads.astype(jnp.float32), query_blk.astype(jnp.float32))
            return (query_part, key_part, value_part)
        query_parts, key_fragments, value_fragments = lax.map(backward_block, positions)
        slice_blocks = BLOCKS_PER_SEQ // N_CTX

        def shard_partial(shard):
            start_index = (shard * slice_blocks).astype(jnp.int32)
            listed_blocks = lax.dynamic_slice_in_dim(block_list, start_index, slice_blocks, 0).reshape(-1)
            key_fragment = lax.dynamic_slice_in_dim(key_fragments, start_index, slice_blocks, 0).reshape(slice_blocks * KEY_SLOTS, BLOCK_SIZE, KEY_VALUE_HEADS * HEAD_DIM)
            value_fragment = lax.dynamic_slice_in_dim(value_fragments, start_index, slice_blocks, 0).reshape(slice_blocks * KEY_SLOTS, BLOCK_SIZE, KEY_VALUE_HEADS * HEAD_DIM)
            key_holder = jnp.zeros((BLOCKS_PER_SEQ, BLOCK_SIZE, KEY_VALUE_HEADS * HEAD_DIM), jnp.float32).at[listed_blocks].add(key_fragment)
            value_holder = jnp.zeros((BLOCKS_PER_SEQ, BLOCK_SIZE, KEY_VALUE_HEADS * HEAD_DIM), jnp.float32).at[listed_blocks].add(value_fragment)
            return (key_holder.astype(jnp.bfloat16), value_holder.astype(jnp.bfloat16))
        key_slices, value_slices = lax.map(shard_partial, jnp.arange(N_CTX, dtype=jnp.int32))
        key_gradient_sum = lax.optimization_barrier(jnp.sum(key_slices.astype(jnp.float32), axis=0)).astype(jnp.bfloat16).reshape(SEQ_LENGTH, KEY_VALUE_HEADS * HEAD_DIM)
        value_gradient_sum = lax.optimization_barrier(jnp.sum(value_slices.astype(jnp.float32), axis=0)).astype(jnp.bfloat16).reshape(SEQ_LENGTH, KEY_VALUE_HEADS * HEAD_DIM)
        return (mixed, query_parts.reshape(SEQ_LENGTH, QUERY_HEADS * HEAD_DIM), key_gradient_sum, value_gradient_sum, out_rows)
    mixed, query_grad, key_grad, value_grad, attended = lax.map(one_sequence, (queries, keys, values, resid, grad_out))
    proj_grad = jnp.dot(attended.reshape(SEQUENCE_COUNT * SEQ_LENGTH, QUERY_HEADS * HEAD_DIM).T, grad_out.reshape(SEQUENCE_COUNT * SEQ_LENGTH, D), preferred_element_type=jnp.float32)
    return (mixed, query_grad, key_grad, value_grad, proj_grad)
```

```python
import functools
import math

import jax
import jax.numpy as jnp
from jax import lax
from jax.experimental import pallas as pl
from jax.experimental.pallas import tpu as pltpu
from jax.sharding import PartitionSpec as P

QUERY_HEADS = 16
KEY_VALUE_HEADS = 4
HEAD_DIM = 128
BLOCK_SIZE = 128
KEY_SLOTS = 8

GROUP = QUERY_HEADS // KEY_VALUE_HEADS
CORE_KV = KEY_VALUE_HEADS // 2
HALF = QUERY_HEADS * HEAD_DIM // 2
KV_HALF = CORE_KV * HEAD_DIM
STACK = GROUP * BLOCK_SIZE
WIDE = GROUP * HEAD_DIM
SCALE = 1.0 / math.sqrt(HEAD_DIM)
EXP2_SCALE = SCALE * math.log2(math.e)
NEG = -1e30
F32 = jnp.float32
BF16 = jnp.bfloat16
VMEM_LIMIT = 56 * 1024 * 1024
NT = (((1,), (1,)), ((), ()))


def dot(a, b):
    return jnp.dot(a, b, preferred_element_type=F32)


def stack_heads(x):
    return jnp.concatenate([x[:, h * HEAD_DIM:(h + 1) * HEAD_DIM] for h in range(GROUP)], axis=0)


def params(steps):
    return pltpu.CompilerParams(dimension_semantics=("arbitrary",) * steps, vmem_limit_bytes=VMEM_LIMIT)


def fill_kv(kv_refs, kv_sc, rows):
    for d, ref in enumerate(kv_refs):
        for u in range(2 * CORE_KV):
            kv_sc[u, d * rows:(d + 1) * rows, :] = ref[:, u * HEAD_DIM:(u + 1) * HEAD_DIM]


def slot_rows(bl_ref, c, i, j, nb):
    b = bl_ref[i, j]
    chip = b // nb
    return pl.multiple_of(((c - chip) * nb + (b - chip * nb)) * BLOCK_SIZE, BLOCK_SIZE)


def allowed_mask(n, count):
    row = lax.broadcasted_iota(jnp.int32, (n, STACK), 0)
    col = lax.broadcasted_iota(jnp.int32, (n, STACK), 1) & (BLOCK_SIZE - 1)
    return row <= jnp.where(row < BLOCK_SIZE, col, count * BLOCK_SIZE - 1)


def by_count(count, run):
    small = KEY_SLOTS // 2

    @pl.when(count <= small)
    def _():
        run(small)

    @pl.when(count > small)
    def _():
        run(KEY_SLOTS)


def forward_kernel(nc, nb, bl_ref, bc_ref, meta_ref, q_ref, *rest):
    kv_refs, (a_ref, at_ref, st_ref, kv_sc) = rest[:nc], rest[nc:]
    g, i = pl.program_id(0), pl.program_id(1)

    @pl.when((g == 0) & (i == 0))
    def _():
        fill_kv(kv_refs, kv_sc, nb * BLOCK_SIZE)

    c = meta_ref[0]
    count = bc_ref[i]

    def run(slots):
        n = slots * BLOCK_SIZE
        starts = [slot_rows(bl_ref, c, i, j, nb) for j in range(slots)]
        qs = stack_heads(q_ref[...])
        k_cat = jnp.concatenate([kv_sc[g, pl.ds(s, BLOCK_SIZE), :] for s in starts], axis=0)
        v_cat = jnp.concatenate([kv_sc[CORE_KV + g, pl.ds(s, BLOCK_SIZE), :] for s in starts], axis=0)
        s_t = lax.dot_general(k_cat, qs, NT, preferred_element_type=F32)
        s_t = jnp.where(allowed_mask(n, count), s_t, NEG)
        top = jnp.max(s_t, axis=0, keepdims=True)
        p = jnp.exp2((s_t - top) * EXP2_SCALE)
        total = jnp.sum(p, axis=0, keepdims=True)
        a_t = dot(v_cat.T, p.astype(BF16)) / total
        st_ref[0, 0] = top * EXP2_SCALE + jnp.log2(total)
        for h in range(GROUP):
            part = a_t[:, h * BLOCK_SIZE:(h + 1) * BLOCK_SIZE]
            at_ref[h * HEAD_DIM:(h + 1) * HEAD_DIM, :] = part.astype(BF16)
            a_ref[:, h * HEAD_DIM:(h + 1) * HEAD_DIM] = part.T.astype(BF16)

    by_count(count, run)


def kv_specs(nc, rows):
    return [pl.BlockSpec((rows, 2 * KV_HALF), lambda g, i, *_: (0, 0)) for _ in range(nc)]


def forward(bl, bc, meta, q, kvs):
    nc, rows = len(kvs), q.shape[0]
    nb = rows // BLOCK_SIZE
    return pl.pallas_call(
        functools.partial(forward_kernel, nc, nb),
        grid_spec=pltpu.PrefetchScalarGridSpec(
            num_scalar_prefetch=3,
            grid=(CORE_KV, nb),
            in_specs=[
                pl.BlockSpec((BLOCK_SIZE, WIDE), lambda g, i, bl, bc, m: (i, m[1] * CORE_KV + g)),
                *kv_specs(nc, rows),
            ],
            out_specs=[
                pl.BlockSpec((BLOCK_SIZE, WIDE), lambda g, i, *_: (i, g)),
                pl.BlockSpec((WIDE, BLOCK_SIZE), lambda g, i, *_: (g, i)),
                pl.BlockSpec((1, 1, 1, STACK), lambda g, i, *_: (g, i, 0, 0)),
            ],
            scratch_shapes=[pltpu.VMEM((2 * CORE_KV, nc * rows, HEAD_DIM), BF16)],
        ),
        out_shape=[
            jax.ShapeDtypeStruct((rows, HALF), BF16),
            jax.ShapeDtypeStruct((HALF, rows), BF16),
            jax.ShapeDtypeStruct((CORE_KV, nb, 1, STACK), F32),
        ],
        compiler_params=params(2),
        cost_estimate=pl.CostEstimate(flops=2_000_000_000, bytes_accessed=4_000_000, transcendentals=2_000_000),
        name="attention_forward",
    )(bl, bc, meta, q, *kvs)


def backward_kernel(nc, nb, bl_ref, bc_ref, meta_ref, q_ref, do_ref, a_ref, st_ref, *rest):
    kv_refs, (dq_ref, dkv_ref, kv_sc, acc) = rest[:nc], rest[nc:]
    g, i = pl.program_id(0), pl.program_id(1)

    @pl.when((g == 0) & (i == 0))
    def _():
        fill_kv(kv_refs, kv_sc, nb * BLOCK_SIZE)

    @pl.when(i == 0)
    def _():
        acc[...] = jnp.zeros_like(acc)

    c = meta_ref[0]
    count = bc_ref[i]

    def run(slots):
        n = slots * BLOCK_SIZE
        starts = [slot_rows(bl_ref, c, i, j, nb) for j in range(slots)]
        qs = stack_heads(q_ref[...])
        dos = stack_heads(do_ref[...])
        outs = stack_heads(a_ref[...])
        row_dot = jnp.sum((dos.astype(F32) * outs.astype(F32)).T, axis=0, keepdims=True)
        k_cat = jnp.concatenate([kv_sc[g, pl.ds(s, BLOCK_SIZE), :] for s in starts], axis=0)
        v_cat = jnp.concatenate([kv_sc[CORE_KV + g, pl.ds(s, BLOCK_SIZE), :] for s in starts], axis=0)
        s_t = lax.dot_general(k_cat, qs, NT, preferred_element_type=F32)
        s_t = jnp.where(allowed_mask(n, count), s_t, NEG)
        p = jnp.exp2(s_t * EXP2_SCALE - st_ref[0, 0])
        dp = lax.dot_general(v_cat, dos, NT, preferred_element_type=F32)
        ds = (p * (dp - row_dot)).astype(BF16)
        dv = dot(p.astype(BF16), dos)
        dk = dot(ds, qs) * SCALE
        dq_t = dot(k_cat.T, ds) * SCALE
        for h in range(GROUP):
            part = dq_t[:, h * BLOCK_SIZE:(h + 1) * BLOCK_SIZE]
            dq_ref[:, h * HEAD_DIM:(h + 1) * HEAD_DIM] = part.T.astype(BF16)
        for j in range(slots):
            at = pl.ds(pl.multiple_of(bl_ref[i, j] * BLOCK_SIZE, BLOCK_SIZE), BLOCK_SIZE)
            acc[0, at, :] += dk[j * BLOCK_SIZE:(j + 1) * BLOCK_SIZE]
            acc[1, at, :] += dv[j * BLOCK_SIZE:(j + 1) * BLOCK_SIZE]

    by_count(count, run)

    @pl.when(i == nb - 1)
    def _():
        dkv_ref[...] = acc[...].astype(BF16)


def backward(bl, bc, meta, q, do, a, st, kvs):
    nc, rows = len(kvs), q.shape[0]
    nb = rows // BLOCK_SIZE
    wide = pl.BlockSpec((BLOCK_SIZE, WIDE), lambda g, i, *_: (i, g))
    return pl.pallas_call(
        functools.partial(backward_kernel, nc, nb),
        grid_spec=pltpu.PrefetchScalarGridSpec(
            num_scalar_prefetch=3,
            grid=(CORE_KV, nb),
            in_specs=[
                pl.BlockSpec((BLOCK_SIZE, WIDE), lambda g, i, bl, bc, m: (i, m[1] * CORE_KV + g)),
                wide,
                wide,
                pl.BlockSpec((1, 1, 1, STACK), lambda g, i, *_: (g, i, 0, 0)),
                *kv_specs(nc, rows),
            ],
            out_specs=[wide, pl.BlockSpec((2, nc * rows, HEAD_DIM), lambda g, i, *_: (0, 0, g))],
            scratch_shapes=[
                pltpu.VMEM((2 * CORE_KV, nc * rows, HEAD_DIM), BF16),
                pltpu.VMEM((2, nc * rows, HEAD_DIM), F32),
            ],
        ),
        out_shape=[
            jax.ShapeDtypeStruct((rows, HALF), BF16),
            jax.ShapeDtypeStruct((2, nc * rows, KV_HALF), BF16),
        ],
        compiler_params=params(2),
        cost_estimate=pl.CostEstimate(flops=6_000_000_000, bytes_accessed=6_000_000, transcendentals=2_000_000),
        name="attention_backward",
    )(bl, bc, meta, q, do, a, st, *kvs)


def column(meta_ref, chip, core, width):
    at = ((meta_ref[2] ^ chip) * 2 + (meta_ref[1] ^ core)) * width
    return pl.ds(pl.multiple_of(at, width), width)


def output_grad_kernel(pieces, width, meta_ref, g0_ref, g1_ref, *rest):
    w_refs, (o0_ref, o1_ref) = rest[:2 * pieces], rest[2 * pieces:]
    grads = jnp.concatenate(
        [
            jnp.concatenate([ref[:, column(meta_ref, chip, core, width)] for ref in (g0_ref, g1_ref)], axis=0)
            for chip in range(pieces)
            for core in range(2)
        ],
        axis=1,
    )
    rows = g0_ref.shape[0]
    for r in range(2):
        refs = w_refs[r * pieces:(r + 1) * pieces]
        w = jnp.concatenate([ref[core] for ref in refs for core in range(2)], axis=1)
        part = lax.dot_general(grads, w, NT, preferred_element_type=F32).astype(BF16)
        span = slice(r * (HALF // 2), (r + 1) * (HALF // 2))
        o0_ref[:, span] = part[:rows]
        o1_ref[:, span] = part[rows:]


def output_grad(meta, g0, g1, w_a, w_b):
    pieces, width, rows = len(w_a), w_a[0].shape[2], g0.shape[0]
    whole = pl.BlockSpec(memory_space=pltpu.VMEM)
    return pl.pallas_call(
        functools.partial(output_grad_kernel, pieces, width),
        in_specs=[pl.BlockSpec(memory_space=pltpu.SMEM)] + [whole] * (2 + 2 * pieces),
        out_specs=[whole, whole],
        out_shape=[jax.ShapeDtypeStruct((rows, HALF), BF16)] * 2,
        compiler_params=params(0),
        cost_estimate=pl.CostEstimate(flops=2_200_000_000, bytes_accessed=8_000_000, transcendentals=0),
        name="output_grad",
    )(meta, g0, g1, *w_a, *w_b)


def mix_kernel(pieces, width, extras, meta_ref, a_ref, *rest):
    w_refs, more, out_ref = rest[:2 * pieces], rest[2 * pieces:-1], rest[-1]
    a = a_ref[...]
    for chip in range(pieces):
        for core in range(2):
            at = column(meta_ref, chip, core, width)
            w = jnp.concatenate([w_refs[chip][core], w_refs[pieces + chip][core]], axis=0)
            part = dot(a, w)
            for ref in more:
                part = part + ref[:, at].astype(F32)
            out_ref[:, at] = part.astype(BF16)


def mix(meta, a, w_a, w_b, more):
    pieces, width, rows = len(w_a), w_a[0].shape[2], a.shape[0]
    whole = pl.BlockSpec(memory_space=pltpu.VMEM)
    return pl.pallas_call(
        functools.partial(mix_kernel, pieces, width, len(more)),
        in_specs=[pl.BlockSpec(memory_space=pltpu.SMEM)] + [whole] * (1 + 2 * pieces + len(more)),
        out_specs=whole,
        out_shape=jax.ShapeDtypeStruct((rows, 2 * pieces * width), BF16),
        compiler_params=params(0),
        cost_estimate=pl.CostEstimate(flops=1_100_000_000, bytes_accessed=8_000_000, transcendentals=0),
        name="mix",
    )(meta, a, *w_a, *w_b, *more)


def proj_kernel(cols_ref, at0_ref, at1_ref, ga0_ref, ga1_ref, gb0_ref, gb1_ref, pa_ref, pb_ref):
    mid = HALF // 2
    at = jnp.concatenate([at0_ref[...], at1_ref[...]], axis=1)
    pa_ref[0] = dot(at[:mid], jnp.concatenate([ga0_ref[...], ga1_ref[...]], axis=0)).astype(BF16)
    pb_ref[0] = dot(at[mid:], jnp.concatenate([gb0_ref[...], gb1_ref[...]], axis=0)).astype(BF16)


def proj_parts(chip, at0, at1, g0, g1, rels_a, rels_b, width):
    rows = g0.shape[0]
    cols = jnp.stack([chip ^ jnp.array(rels_a, jnp.int32), chip ^ jnp.array(rels_b, jnp.int32)])
    count = len(rels_a)
    turned = pl.BlockSpec((HALF, rows), lambda j, c: (0, 0))
    grad_a = pl.BlockSpec((rows, width), lambda j, c: (0, c[0, j]))
    grad_b = pl.BlockSpec((rows, width), lambda j, c: (0, c[1, j]))
    out = pl.BlockSpec((1, HALF // 2, width), lambda j, c: (j, 0, 0))
    return pl.pallas_call(
        proj_kernel,
        grid_spec=pltpu.PrefetchScalarGridSpec(
            num_scalar_prefetch=1,
            grid=(count,),
            in_specs=[turned, turned, grad_a, grad_a, grad_b, grad_b],
            out_specs=[out, out],
        ),
        out_shape=[jax.ShapeDtypeStruct((count, HALF // 2, width), BF16)] * 2,
        compiler_params=params(1),
        cost_estimate=pl.CostEstimate(flops=1_100_000_000, bytes_accessed=4_000_000, transcendentals=0),
        name="proj_parts",
    )(cols, at0, at1, g0, g1, g0, g1)


def local(nc, nf, queries, keys, values, resid, grad_out, w_out, block_list, block_count):
    chips = nf // 2
    bits = [1 << b for b in range(chips.bit_length() - 1)]
    routes = (bits, bits[::-1])
    c = lax.axis_index("ctx")
    f = lax.axis_index("fsdp")
    core, chip = f % 2, f // 2
    meta = jnp.stack([c, core, chip]).astype(jnp.int32)
    rows = queries.shape[1]
    width = w_out.shape[1]

    def to_core(x):
        return lax.ppermute(x, "fsdp", [(p, p ^ 1) for p in range(nf)])

    def to_chip(x, bit):
        return lax.ppermute(x, "fsdp", [(p, p ^ (2 * bit)) for p in range(nf)])

    def place(mine, theirs, axis):
        return jnp.where(
            core == 0,
            jnp.concatenate([mine, theirs], axis=axis),
            jnp.concatenate([theirs, mine], axis=axis),
        )

    def kv_part(k, v):
        cut = lambda x: lax.dynamic_slice_in_dim(x, core * KV_HALF, KV_HALF, 1)
        return jnp.concatenate([cut(k), cut(v)], axis=1)

    q0, g0 = queries[0], grad_out[0]
    w_mine = lax.dynamic_slice_in_dim(w_out, core * HALF, HALF, 0)
    w_theirs = to_core(lax.dynamic_slice_in_dim(w_out, (1 - core) * HALF, HALF, 0))
    kv0 = kv_part(keys[0], values[0])
    kv1 = kv_part(to_core(keys[0]), to_core(values[0]))
    g1, q1 = to_core(g0), to_core(q0)

    def chain_up(x):
        got = [x]
        for step in range(1, nc):
            got.append(lax.ppermute(got[-1], "ctx", [(p, p + 1) for p in range(step - 1, nc - 1)]))
        return got

    kvs0, kvs1 = chain_up(kv0), chain_up(kv1)

    def gather_w(r):
        span = slice(r * (HALF // 2), (r + 1) * (HALF // 2))
        blocks = {0: jnp.stack([w_mine[span], w_theirs[span]])}
        for bit in routes[r]:
            blocks.update({rel ^ bit: to_chip(x, bit) for rel, x in list(blocks.items())})
        return [blocks[rel] for rel in range(chips)]

    w_a, w_b = gather_w(0), gather_w(1)

    a0, at0, st0 = forward(block_list, block_count, meta, q0, kvs0)
    a1, at1, st1 = forward(block_list, block_count, meta, q1, kvs1)

    with_bit = [[rel for rel in range(chips) if rel & route[0]] for route in routes]
    without = [[rel for rel in range(chips) if not rel & route[0]] for route in routes]
    sent = proj_parts(chip, at0, at1, g0, g1, with_bit[0], with_bit[1], 2 * width)
    kept = proj_parts(chip, at0, at1, g0, g1, without[0], without[1], 2 * width)
    do0, do1 = output_grad(meta, g0, g1, w_a, w_b)

    dq1, dkv1 = backward(block_list, block_count, meta, q1, do1, a1, st1, kvs1)
    dq0, dkv0 = backward(block_list, block_count, meta, q0, do0, a0, st0, kvs0)

    def chain_down(dkv):
        def shard(t):
            return lax.dynamic_slice_in_dim(dkv, jnp.maximum(t, 0) * rows, rows, 1)

        carry = shard(c + 1 - nc)
        for step in range(1, nc):
            got = lax.ppermute(carry, "ctx", [(p, p - 1) for p in range(max(nc - step, 1), nc)])
            own = shard(c + step + 1 - nc)
            carry = (own.astype(F32) + got.astype(F32)).astype(BF16)
        return carry

    sum1 = chain_down(dkv1)
    sum0 = chain_down(dkv0)

    def reduce_chips(r):
        have = {rel: kept[r][n] for n, rel in enumerate(without[r])}
        got = to_chip(sent[r], routes[r][0])
        have = {
            rel: have[rel].astype(F32) + got[n].astype(F32)
            for n, rel in enumerate(rel ^ routes[r][0] for rel in with_bit[r])
        }
        for bit in routes[r][1:]:
            far = [rel for rel in have if rel & bit]
            got = to_chip(jnp.stack([have[rel].astype(BF16) for rel in far]), bit)
            have = {rel ^ bit: have[rel ^ bit] + got[n].astype(F32) for n, rel in enumerate(far)}
        return have[0].astype(BF16)

    proj = jnp.concatenate([reduce_chips(0), reduce_chips(1)], axis=0)
    proj_mine = lax.dynamic_slice_in_dim(proj, core * width, width, 1)
    proj_theirs = to_core(lax.dynamic_slice_in_dim(proj, (1 - core) * width, width, 1))
    proj_rows = place(proj_mine, proj_theirs, 0)
    proj_grad = lax.psum_scatter(proj_rows, "ctx", scatter_dimension=0, tiled=True).astype(F32)

    mixed = mix(meta, a0, w_a, w_b, [resid[0], to_core(mix(meta, a1, w_a, w_b, []))])
    query_grad = place(dq0, to_core(dq1), 1)
    grads = place(sum0, to_core(sum1), 2)
    return mixed[None], query_grad[None], grads[:1], grads[1:], proj_grad


def solution(mesh):
    rows = P("fsdp", "ctx", None)
    body = functools.partial(local, mesh.shape["ctx"], mesh.shape["fsdp"])
    return jax.shard_map(
        body,
        mesh=mesh,
        in_specs=(rows, rows, rows, rows, rows, P(None, "fsdp"), P("ctx", None), P("ctx")),
        out_specs=(rows, rows, rows, rows, P("ctx", "fsdp")),
        check_vma=False,
    )
```

```python
import functools
import math

import jax
import jax.numpy as jnp
from jax import lax
from jax.experimental import pallas as pl
from jax.experimental.pallas import tpu as pltpu
from jax.sharding import PartitionSpec as P

QUERY_HEADS = 16
KEY_VALUE_HEADS = 4
HEAD_DIM = 128
BLOCK_SIZE = 128
KEY_SLOTS = 8

GROUP = QUERY_HEADS // KEY_VALUE_HEADS
CORE_KV = KEY_VALUE_HEADS // 2
HALF = QUERY_HEADS * HEAD_DIM // 2
KV_HALF = CORE_KV * HEAD_DIM
STACK = GROUP * BLOCK_SIZE
WIDE = GROUP * HEAD_DIM
SCALE = 1.0 / math.sqrt(HEAD_DIM)
EXP2_SCALE = SCALE * math.log2(math.e)
NEG = -1e30
F32 = jnp.float32
BF16 = jnp.bfloat16
VMEM_LIMIT = 56 * 1024 * 1024
NT = (((1,), (1,)), ((), ()))


def dot(a, b):
    return jnp.dot(a, b, preferred_element_type=F32)


def stack_heads(x):
    return jnp.concatenate([x[:, h * HEAD_DIM:(h + 1) * HEAD_DIM] for h in range(GROUP)], axis=0)


def params(steps):
    return pltpu.CompilerParams(dimension_semantics=("arbitrary",) * steps, vmem_limit_bytes=VMEM_LIMIT)


def fill_kv(kv_refs, kv_sc, rows):
    for d, ref in enumerate(kv_refs):
        for u in range(2 * CORE_KV):
            kv_sc[u, d * rows:(d + 1) * rows, :] = ref[:, u * HEAD_DIM:(u + 1) * HEAD_DIM]


def slot_rows(bl_ref, c, i, j, nb):
    b = bl_ref[i, j]
    chip = b // nb
    return pl.multiple_of(((c - chip) * nb + (b - chip * nb)) * BLOCK_SIZE, BLOCK_SIZE)


def allowed_mask(n, count):
    row = lax.broadcasted_iota(jnp.int32, (n, STACK), 0)
    col = lax.broadcasted_iota(jnp.int32, (n, STACK), 1) & (BLOCK_SIZE - 1)
    return row <= jnp.where(row < BLOCK_SIZE, col, count * BLOCK_SIZE - 1)


def by_count(count, run):
    small = KEY_SLOTS // 2

    @pl.when(count <= small)
    def _():
        run(small)

    @pl.when(count > small)
    def _():
        run(KEY_SLOTS)


def forward_kernel(nc, nb, bl_ref, bc_ref, meta_ref, q_ref, *rest):
    kv_refs, (a_ref, at_ref, st_ref, kv_sc) = rest[:nc], rest[nc:]
    g, i = pl.program_id(0), pl.program_id(1)

    @pl.when((g == 0) & (i == 0))
    def _():
        fill_kv(kv_refs, kv_sc, nb * BLOCK_SIZE)

    c = meta_ref[0]
    count = bc_ref[i]

    def run(slots):
        n = slots * BLOCK_SIZE
        starts = [slot_rows(bl_ref, c, i, j, nb) for j in range(slots)]
        qs = stack_heads(q_ref[...])
        k_cat = jnp.concatenate([kv_sc[g, pl.ds(s, BLOCK_SIZE), :] for s in starts], axis=0)
        v_cat = jnp.concatenate([kv_sc[CORE_KV + g, pl.ds(s, BLOCK_SIZE), :] for s in starts], axis=0)
        s_t = lax.dot_general(k_cat, qs, NT, preferred_element_type=F32)
        s_t = jnp.where(allowed_mask(n, count), s_t, NEG)
        top = jnp.max(s_t, axis=0, keepdims=True)
        p = jnp.exp2((s_t - top) * EXP2_SCALE)
        total = jnp.sum(p, axis=0, keepdims=True)
        a_t = dot(v_cat.T, p.astype(BF16)) / total
        st_ref[0, 0] = top * EXP2_SCALE + jnp.log2(total)
        for h in range(GROUP):
            part = a_t[:, h * BLOCK_SIZE:(h + 1) * BLOCK_SIZE]
            at_ref[h * HEAD_DIM:(h + 1) * HEAD_DIM, :] = part.astype(BF16)
            a_ref[:, h * HEAD_DIM:(h + 1) * HEAD_DIM] = part.T.astype(BF16)

    by_count(count, run)


def kv_specs(nc, rows):
    return [pl.BlockSpec((rows, 2 * KV_HALF), lambda g, i, *_: (0, 0)) for _ in range(nc)]


def forward(bl, bc, meta, q, kvs):
    nc, rows = len(kvs), q.shape[0]
    nb = rows // BLOCK_SIZE
    return pl.pallas_call(
        functools.partial(forward_kernel, nc, nb),
        grid_spec=pltpu.PrefetchScalarGridSpec(
            num_scalar_prefetch=3,
            grid=(CORE_KV, nb),
            in_specs=[
                pl.BlockSpec((BLOCK_SIZE, WIDE), lambda g, i, bl, bc, m: (i, m[1] * CORE_KV + g)),
                *kv_specs(nc, rows),
            ],
            out_specs=[
                pl.BlockSpec((BLOCK_SIZE, WIDE), lambda g, i, *_: (i, g)),
                pl.BlockSpec((WIDE, BLOCK_SIZE), lambda g, i, *_: (g, i)),
                pl.BlockSpec((1, 1, 1, STACK), lambda g, i, *_: (g, i, 0, 0)),
            ],
            scratch_shapes=[pltpu.VMEM((2 * CORE_KV, nc * rows, HEAD_DIM), BF16)],
        ),
        out_shape=[
            jax.ShapeDtypeStruct((rows, HALF), BF16),
            jax.ShapeDtypeStruct((HALF, rows), BF16),
            jax.ShapeDtypeStruct((CORE_KV, nb, 1, STACK), F32),
        ],
        compiler_params=params(2),
        cost_estimate=pl.CostEstimate(flops=2_000_000_000, bytes_accessed=4_000_000, transcendentals=2_000_000),
        name="attention_forward",
    )(bl, bc, meta, q, *kvs)


def backward_kernel(nc, nb, bl_ref, bc_ref, meta_ref, q_ref, do_ref, a_ref, st_ref, *rest):
    kv_refs, (dq_ref, dkv_ref, kv_sc, acc) = rest[:nc], rest[nc:]
    g, i = pl.program_id(0), pl.program_id(1)

    @pl.when((g == 0) & (i == 0))
    def _():
        fill_kv(kv_refs, kv_sc, nb * BLOCK_SIZE)

    @pl.when(i == 0)
    def _():
        acc[...] = jnp.zeros_like(acc)

    c = meta_ref[0]
    count = bc_ref[i]

    def run(slots):
        n = slots * BLOCK_SIZE
        starts = [slot_rows(bl_ref, c, i, j, nb) for j in range(slots)]
        qs = stack_heads(q_ref[...])
        dos = stack_heads(do_ref[...])
        outs = stack_heads(a_ref[...])
        row_dot = jnp.sum((dos.astype(F32) * outs.astype(F32)).T, axis=0, keepdims=True)
        k_cat = jnp.concatenate([kv_sc[g, pl.ds(s, BLOCK_SIZE), :] for s in starts], axis=0)
        v_cat = jnp.concatenate([kv_sc[CORE_KV + g, pl.ds(s, BLOCK_SIZE), :] for s in starts], axis=0)
        s_t = lax.dot_general(k_cat, qs, NT, preferred_element_type=F32)
        s_t = jnp.where(allowed_mask(n, count), s_t, NEG)
        p = jnp.exp2(s_t * EXP2_SCALE - st_ref[0, 0])
        dp = lax.dot_general(v_cat, dos, NT, preferred_element_type=F32)
        ds = (p * (dp - row_dot)).astype(BF16)
        dv = dot(p.astype(BF16), dos)
        dk = dot(ds, qs) * SCALE
        dq_t = dot(k_cat.T, ds) * SCALE
        for h in range(GROUP):
            part = dq_t[:, h * BLOCK_SIZE:(h + 1) * BLOCK_SIZE]
            dq_ref[:, h * HEAD_DIM:(h + 1) * HEAD_DIM] = part.T.astype(BF16)
        for j in range(slots):
            at = pl.ds(pl.multiple_of(bl_ref[i, j] * BLOCK_SIZE, BLOCK_SIZE), BLOCK_SIZE)
            acc[0, at, :] += dk[j * BLOCK_SIZE:(j + 1) * BLOCK_SIZE]
            acc[1, at, :] += dv[j * BLOCK_SIZE:(j + 1) * BLOCK_SIZE]

    by_count(count, run)

    @pl.when(i == nb - 1)
    def _():
        dkv_ref[...] = acc[...].astype(BF16)


def backward(bl, bc, meta, q, do, a, st, kvs):
    nc, rows = len(kvs), q.shape[0]
    nb = rows // BLOCK_SIZE
    wide = pl.BlockSpec((BLOCK_SIZE, WIDE), lambda g, i, *_: (i, g))
    return pl.pallas_call(
        functools.partial(backward_kernel, nc, nb),
        grid_spec=pltpu.PrefetchScalarGridSpec(
            num_scalar_prefetch=3,
            grid=(CORE_KV, nb),
            in_specs=[
                pl.BlockSpec((BLOCK_SIZE, WIDE), lambda g, i, bl, bc, m: (i, m[1] * CORE_KV + g)),
                wide,
                wide,
                pl.BlockSpec((1, 1, 1, STACK), lambda g, i, *_: (g, i, 0, 0)),
                *kv_specs(nc, rows),
            ],
            out_specs=[wide, pl.BlockSpec((2, nc * rows, HEAD_DIM), lambda g, i, *_: (0, 0, g))],
            scratch_shapes=[
                pltpu.VMEM((2 * CORE_KV, nc * rows, HEAD_DIM), BF16),
                pltpu.VMEM((2, nc * rows, HEAD_DIM), F32),
            ],
        ),
        out_shape=[
            jax.ShapeDtypeStruct((rows, HALF), BF16),
            jax.ShapeDtypeStruct((2, nc * rows, KV_HALF), BF16),
        ],
        compiler_params=params(2),
        cost_estimate=pl.CostEstimate(flops=6_000_000_000, bytes_accessed=6_000_000, transcendentals=2_000_000),
        name="attention_backward",
    )(bl, bc, meta, q, do, a, st, *kvs)


def column(meta_ref, chip, core, width):
    at = ((meta_ref[2] ^ chip) * 2 + (meta_ref[1] ^ core)) * width
    return pl.ds(pl.multiple_of(at, width), width)


def read_piece(w_refs, piece):
    ref, lead, start = piece
    rows = pl.ds(start, HALF // 2)
    return w_refs[ref][rows, :] if lead is None else w_refs[ref][lead, rows, :]


def output_grad_kernel(plan, width, meta_ref, g0_ref, g1_ref, *rest):
    w_refs, (o0_ref, o1_ref) = rest[:-2], rest[-2:]
    grads = jnp.concatenate(
        [
            jnp.concatenate([ref[:, column(meta_ref, chip, core, width)] for ref in (g0_ref, g1_ref)], axis=0)
            for chip, core, _ in plan
        ],
        axis=1,
    )
    rows = g0_ref.shape[0]
    for r in range(2):
        w = jnp.concatenate([read_piece(w_refs, pieces[r]) for _, _, pieces in plan], axis=1)
        part = lax.dot_general(grads, w, NT, preferred_element_type=F32).astype(BF16)
        span = slice(r * (HALF // 2), (r + 1) * (HALF // 2))
        o0_ref[:, span] = part[:rows]
        o1_ref[:, span] = part[rows:]


def output_grad(meta, g0, g1, plan, arrays):
    width, rows = arrays[0].shape[-1], g0.shape[0]
    whole = pl.BlockSpec(memory_space=pltpu.VMEM)
    return pl.pallas_call(
        functools.partial(output_grad_kernel, plan, width),
        in_specs=[pl.BlockSpec(memory_space=pltpu.SMEM)] + [whole] * (2 + len(arrays)),
        out_specs=[whole, whole],
        out_shape=[jax.ShapeDtypeStruct((rows, HALF), BF16)] * 2,
        compiler_params=params(0),
        cost_estimate=pl.CostEstimate(flops=2_200_000_000, bytes_accessed=8_000_000, transcendentals=0),
        name="output_grad",
    )(meta, g0, g1, *arrays)


def mix_kernel(plan, width, count, meta_ref, a_ref, *rest):
    w_refs, more, out_ref = rest[:count], rest[count:-1], rest[-1]
    a = a_ref[...]
    for chip, core, pieces in plan:
        at = column(meta_ref, chip, core, width)
        part = dot(a, jnp.concatenate([read_piece(w_refs, piece) for piece in pieces], axis=0))
        for ref in more:
            part = part + ref[:, at].astype(F32)
        out_ref[:, at] = part.astype(BF16)


def mix(meta, a, plan, arrays, more):
    width, rows = arrays[0].shape[-1], a.shape[0]
    whole = pl.BlockSpec(memory_space=pltpu.VMEM)
    return pl.pallas_call(
        functools.partial(mix_kernel, plan, width, len(arrays)),
        in_specs=[pl.BlockSpec(memory_space=pltpu.SMEM)] + [whole] * (1 + len(arrays) + len(more)),
        out_specs=whole,
        out_shape=jax.ShapeDtypeStruct((rows, len(plan) * width), BF16),
        compiler_params=params(0),
        cost_estimate=pl.CostEstimate(flops=1_100_000_000, bytes_accessed=8_000_000, transcendentals=0),
        name="mix",
    )(meta, a, *arrays, *more)


def proj_kernel(cols_ref, at0_ref, at1_ref, ga0_ref, ga1_ref, gb0_ref, gb1_ref, pa_ref, pb_ref):
    mid = HALF // 2
    at = jnp.concatenate([at0_ref[...], at1_ref[...]], axis=1)
    pa_ref[0] = dot(at[:mid], jnp.concatenate([ga0_ref[...], ga1_ref[...]], axis=0)).astype(BF16)
    pb_ref[0] = dot(at[mid:], jnp.concatenate([gb0_ref[...], gb1_ref[...]], axis=0)).astype(BF16)


def proj_parts(chip, at0, at1, g0, g1, rels_a, rels_b, width):
    rows = g0.shape[0]
    cols = jnp.stack([chip ^ jnp.array(rels_a, jnp.int32), chip ^ jnp.array(rels_b, jnp.int32)])
    count = len(rels_a)
    turned = pl.BlockSpec((HALF, rows), lambda j, c: (0, 0))
    grad_a = pl.BlockSpec((rows, width), lambda j, c: (0, c[0, j]))
    grad_b = pl.BlockSpec((rows, width), lambda j, c: (0, c[1, j]))
    out = pl.BlockSpec((1, HALF // 2, width), lambda j, c: (j, 0, 0))
    return pl.pallas_call(
        proj_kernel,
        grid_spec=pltpu.PrefetchScalarGridSpec(
            num_scalar_prefetch=1,
            grid=(count,),
            in_specs=[turned, turned, grad_a, grad_a, grad_b, grad_b],
            out_specs=[out, out],
        ),
        out_shape=[jax.ShapeDtypeStruct((count, HALF // 2, width), BF16)] * 2,
        compiler_params=params(1),
        cost_estimate=pl.CostEstimate(flops=1_100_000_000, bytes_accessed=4_000_000, transcendentals=0),
        name="proj_parts",
    )(cols, at0, at1, g0, g1, g0, g1)


def after(x, *earlier):
    return lax.optimization_barrier((x, *earlier))[0]


def local(nc, nf, queries, keys, values, resid, grad_out, w_out, block_list, block_count):
    chips = nf // 2
    bits = [1 << b for b in range(chips.bit_length() - 1)]
    routes = (bits, bits[::-1])
    mid = HALF // 2
    c = lax.axis_index("ctx")
    f = lax.axis_index("fsdp")
    core, chip = f % 2, f // 2
    meta = jnp.stack([c, core, chip]).astype(jnp.int32)
    rows = queries.shape[1]
    width = w_out.shape[1]

    def to_core(x):
        return lax.ppermute(x, "fsdp", [(p, p ^ 1) for p in range(nf)])

    def to_chip(x, bit):
        return lax.ppermute(x, "fsdp", [(p, p ^ (2 * bit)) for p in range(nf)])

    def place(mine, theirs, axis):
        return jnp.where(
            core == 0,
            jnp.concatenate([mine, theirs], axis=axis),
            jnp.concatenate([theirs, mine], axis=axis),
        )

    def kv_part(which):
        cut = lambda x: lax.dynamic_slice_in_dim(x[0], which * KV_HALF, KV_HALF, 1)
        return jnp.concatenate([cut(keys), cut(values)], axis=1)

    def chain_up(x):
        got = [x]
        for step in range(1, nc):
            got.append(lax.ppermute(got[-1], "ctx", [(p, p + 1) for p in range(step - 1, nc - 1)]))
        return got

    q0, g0 = queries[0], grad_out[0]
    kv1 = to_core(kv_part(1 - core))
    kvs0 = chain_up(kv_part(core))
    kvs1 = chain_up(kv1)
    w_mine = lax.dynamic_slice_in_dim(w_out, core * HALF, HALF, 0)
    w_theirs = to_core(lax.dynamic_slice_in_dim(w_out, (1 - core) * HALF, HALF, 0))
    g1 = to_core(after(g0, w_theirs, kv1))
    q1 = to_core(after(q0, g1))

    arrays = [w_mine, w_theirs]
    held = {(0, core_bit, r): (core_bit, None, r * mid) for core_bit in range(2) for r in range(2)}
    link_last = {}
    for bit in bits:
        first = to_chip(w_mine, bit)
        link_last[bit] = to_chip(after(w_theirs, first), bit)
        for core_bit, x in enumerate((first, link_last[bit])):
            for r in range(2):
                held[bit, core_bit, r] = (len(arrays), None, r * mid)
            arrays.append(x)
    for step in range(1, len(bits)):
        for r in range(2):
            bit = routes[r][step]
            known = [0]
            for done in routes[r][:step]:
                known += [rel ^ done for rel in known]
            sources = [(rel, core_bit) for rel in known[1:] for core_bit in range(2)]
            parts = []
            for source in sources:
                ref, lead, start = held[(*source, r)]
                x = arrays[ref] if lead is None else arrays[ref][lead]
                parts.append(x[start:start + mid])
            link_last[bit] = to_chip(after(jnp.stack(parts), link_last[bit]), bit)
            for n, (rel, core_bit) in enumerate(sources):
                held[rel ^ bit, core_bit, r] = (len(arrays), n, 0)
            arrays.append(link_last[bit])
    plan = [
        (rel, core_bit, [held[rel, core_bit, r] for r in range(2)]) for rel in range(chips) for core_bit in range(2)
    ]

    a0, at0, st0 = forward(block_list, block_count, meta, q0, kvs0)
    a1, at1, st1 = forward(block_list, block_count, meta, q1, kvs1)

    with_bit = [[rel for rel in range(chips) if rel & route[0]] for route in routes]
    without = [[rel for rel in range(chips) if not rel & route[0]] for route in routes]
    sent = proj_parts(chip, at0, at1, g0, g1, with_bit[0], with_bit[1], 2 * width)
    do0, do1 = output_grad(meta, g0, g1, plan, arrays)
    dq1, dkv1 = backward(block_list, block_count, meta, q1, do1, a1, st1, kvs1)
    dq0, dkv0 = backward(block_list, block_count, meta, q0, do0, a0, st0, kvs0)
    kept = proj_parts(chip, at0, at1, g0, g1, without[0], without[1], 2 * width)

    def add(x, y):
        return (x.astype(F32) + y.astype(F32)).astype(BF16)

    def chain_down(shard):
        carry = shard(jnp.maximum(c + 1 - nc, 0))
        for step in range(1, nc):
            got = lax.ppermute(carry, "ctx", [(p, p - 1) for p in range(max(nc - step, 1), nc)])
            if step < nc - 1:
                carry = add(shard(jnp.maximum(c + step + 1 - nc, 0)), got)
        return got

    def chain_out(shard):
        carry = shard(jnp.minimum(c + nc - 1, nc - 1))
        for step in range(1, nc):
            got = lax.ppermute(carry, "ctx", [(p, p + 1) for p in range(min(step, nc - 1))])
            if step < nc - 1:
                carry = add(shard(jnp.minimum(c + nc - 1 - step, nc - 1)), got)
        return got

    def kv_sum(dkv):
        shard = lambda t: lax.dynamic_slice_in_dim(dkv, t * rows, rows, 1)
        return add(shard(c), chain_down(shard))

    sum1 = kv_sum(dkv1)
    sum0 = kv_sum(dkv0)

    def reduce_chips(r):
        have = {rel: kept[r][n] for n, rel in enumerate(without[r])}
        got = to_chip(sent[r], routes[r][0])
        have = {
            rel: have[rel].astype(F32) + got[n].astype(F32)
            for n, rel in enumerate(rel ^ routes[r][0] for rel in with_bit[r])
        }
        for bit in routes[r][1:]:
            far = [rel for rel in have if rel & bit]
            got = to_chip(jnp.stack([have[rel].astype(BF16) for rel in far]), bit)
            have = {rel ^ bit: have[rel ^ bit] + got[n].astype(F32) for n, rel in enumerate(far)}
        return have[0].astype(BF16)

    proj = jnp.concatenate([reduce_chips(0), reduce_chips(1)], axis=0)
    proj_mine = lax.dynamic_slice_in_dim(proj, core * width, width, 1)
    proj_theirs = to_core(lax.dynamic_slice_in_dim(proj, (1 - core) * width, width, 1))
    proj_rows = place(proj_mine, proj_theirs, 0)
    share = QUERY_HEADS * HEAD_DIM // nc
    proj_shard = lambda t: lax.dynamic_slice_in_dim(proj_rows, t * share, share, 0)
    proj_grad = (
        proj_shard(c).astype(F32) + chain_down(proj_shard).astype(F32) + chain_out(proj_shard).astype(F32)
    )

    mixed = mix(meta, a0, plan, arrays, [resid[0], to_core(mix(meta, a1, plan, arrays, []))])
    query_grad = place(dq0, to_core(dq1), 1)
    grads = place(sum0, to_core(sum1), 2)
    return mixed[None], query_grad[None], grads[:1], grads[1:], proj_grad


def solution(mesh):
    rows = P("fsdp", "ctx", None)
    body = functools.partial(local, mesh.shape["ctx"], mesh.shape["fsdp"])
    return jax.shard_map(
        body,
        mesh=mesh,
        in_specs=(rows, rows, rows, rows, rows, P(None, "fsdp"), P("ctx", None), P("ctx")),
        out_specs=(rows, rows, rows, rows, P("ctx", "fsdp")),
        check_vma=False,
    )
```

```python
import functools
import math

import jax
import jax.numpy as jnp
from jax import lax
from jax.experimental import pallas as pl
from jax.experimental.pallas import tpu as pltpu
from jax.sharding import PartitionSpec as P

QUERY_HEADS = 16
KEY_VALUE_HEADS = 4
HEAD_DIM = 128
BLOCK_SIZE = 128
KEY_SLOTS = 8

GROUP = QUERY_HEADS // KEY_VALUE_HEADS
CORE_KV = KEY_VALUE_HEADS // 2
HALF = QUERY_HEADS * HEAD_DIM // 2
KV_HALF = CORE_KV * HEAD_DIM
STACK = GROUP * BLOCK_SIZE
WIDE = GROUP * HEAD_DIM
SCALE = 1.0 / math.sqrt(HEAD_DIM)
EXP2_SCALE = SCALE * math.log2(math.e)
NEG = -1e30
F32 = jnp.float32
BF16 = jnp.bfloat16
VMEM_LIMIT = 56 * 1024 * 1024
NT = (((1,), (1,)), ((), ()))


def dot(a, b):
    return jnp.dot(a, b, preferred_element_type=F32)


def stack_heads(x):
    return jnp.concatenate([x[:, h * HEAD_DIM:(h + 1) * HEAD_DIM] for h in range(GROUP)], axis=0)


def cost(weight):
    return pl.CostEstimate(flops=int(weight * 1e9), bytes_accessed=1_000_000, transcendentals=0)


def params(steps):
    return pltpu.CompilerParams(dimension_semantics=("arbitrary",) * steps, vmem_limit_bytes=VMEM_LIMIT)


def fill_kv(kv_refs, kv_sc, rows, nc):
    for n, ref in enumerate(kv_refs):
        d = n % nc
        for u in range(2 * CORE_KV):
            kv_sc[n // nc, u, d * rows:(d + 1) * rows, :] = ref[:, u * HEAD_DIM:(u + 1) * HEAD_DIM]


def slot_rows(bl_ref, c, i, j, nb):
    b = bl_ref[i, j]
    chip = b // nb
    return pl.multiple_of(((c - chip) * nb + (b - chip * nb)) * BLOCK_SIZE, BLOCK_SIZE)


def masked_scores(k_cat, qs, slots, count):
    s_t = lax.dot_general(k_cat, qs, NT, preferred_element_type=F32)
    key = lax.broadcasted_iota(jnp.int32, (BLOCK_SIZE, STACK), 0)
    query = lax.broadcasted_iota(jnp.int32, (BLOCK_SIZE, STACK), 1) & (BLOCK_SIZE - 1)
    parts = [jnp.where(key <= query, s_t[:BLOCK_SIZE], NEG)]
    for j in range(1, slots):
        parts.append(jnp.where(j < count, s_t[j * BLOCK_SIZE:(j + 1) * BLOCK_SIZE], NEG))
    return jnp.concatenate(parts, axis=0)


def by_count(count, run):
    small = KEY_SLOTS // 2

    @pl.when(count <= small)
    def _():
        run(small)

    @pl.when(count > small)
    def _():
        run(KEY_SLOTS)


def wide_part(ref, g):
    return stack_heads(ref[0, :, g * WIDE:(g + 1) * WIDE])


def slot_cat(kv_sc, s, u, starts):
    return jnp.concatenate([kv_sc[s, u, pl.ds(at, BLOCK_SIZE), :] for at in starts], axis=0)


def forward_kernel(nc, nb, bl_ref, bc_ref, meta_ref, q_ref, *rest):
    kv_refs, (a_ref, *at_refs, st_ref, kv_sc) = rest[:2 * nc], rest[2 * nc:]
    step = pl.program_id(0)
    s, i = step // nb, step % nb

    @pl.when(step == 0)
    def _():
        fill_kv(kv_refs, kv_sc, nb * BLOCK_SIZE, nc)

    c = meta_ref[0]
    count = bc_ref[i]

    def run(slots):
        starts = [slot_rows(bl_ref, c, i, j, nb) for j in range(slots)]
        for g in range(CORE_KV):
            qs = wide_part(q_ref, g)
            k_cat = slot_cat(kv_sc, s, g, starts)
            v_cat = slot_cat(kv_sc, s, CORE_KV + g, starts)
            s_t = masked_scores(k_cat, qs, slots, count)
            top = jnp.max(s_t, axis=0, keepdims=True)
            p = jnp.exp2((s_t - top) * EXP2_SCALE)
            total = jnp.sum(p, axis=0, keepdims=True)
            a_t = dot(v_cat.T, p.astype(BF16)) / total
            st_ref[0, g] = top * EXP2_SCALE + jnp.log2(total)
            for h in range(GROUP):
                part = a_t[:, h * BLOCK_SIZE:(h + 1) * BLOCK_SIZE]
                at_refs[g][0, h * HEAD_DIM:(h + 1) * HEAD_DIM, :] = part.astype(BF16)
                lane = g * WIDE + h * HEAD_DIM
                a_ref[0, :, lane:lane + HEAD_DIM] = part.T.astype(BF16)

    by_count(count, run)


def kv_specs(nc, rows):
    return [pl.BlockSpec((rows, 2 * KV_HALF), lambda n, *_: (0, 0)) for _ in range(2 * nc)]


def forward(bl, bc, meta, q, kvs, weight=20):
    nc, rows = len(kvs) // 2, q.shape[1]
    nb = rows // BLOCK_SIZE
    wide = pl.BlockSpec((1, BLOCK_SIZE, HALF), lambda n, *_: (n // nb, n % nb, 0))
    turned = pl.BlockSpec((1, WIDE, BLOCK_SIZE), lambda n, *_: (n // nb, 0, n % nb))
    return pl.pallas_call(
        functools.partial(forward_kernel, nc, nb),
        grid_spec=pltpu.PrefetchScalarGridSpec(
            num_scalar_prefetch=3,
            grid=(2 * nb,),
            in_specs=[wide, *kv_specs(nc, rows)],
            out_specs=[wide, *[turned] * CORE_KV, pl.BlockSpec((1, CORE_KV, 1, STACK), lambda n, *_: (n, 0, 0, 0))],
            scratch_shapes=[pltpu.VMEM((2, 2 * CORE_KV, nc * rows, HEAD_DIM), BF16)],
        ),
        out_shape=[
            jax.ShapeDtypeStruct((2, rows, HALF), BF16),
            *[jax.ShapeDtypeStruct((2, WIDE, rows), BF16)] * CORE_KV,
            jax.ShapeDtypeStruct((2 * nb, CORE_KV, 1, STACK), F32),
        ],
        compiler_params=params(1),
        cost_estimate=cost(weight),
        name="attention_forward",
    )(bl, bc, meta, q, *kvs)


def backward_kernel(nc, nb, plan, width, bl_ref, bc_ref, meta_ref, q_ref, a_ref, st_ref, g0_ref, g1_ref, *rest):
    kv_refs, w_refs, (dq_ref, dkv_ref, kv_sc, do_sc, acc) = rest[:2 * nc], rest[2 * nc:-5], rest[-5:]
    step = pl.program_id(0)
    s, i = step // nb, step % nb
    rows = nb * BLOCK_SIZE

    @pl.when(step == 0)
    def _():
        for span, part in output_grad_product(plan, width, meta_ref, (g0_ref, g1_ref), w_refs):
            do_sc[0, :, span] = part[:rows].astype(BF16)
            do_sc[1, :, span] = part[rows:].astype(BF16)
        fill_kv(kv_refs, kv_sc, rows, nc)

    @pl.when(i == 0)
    def _():
        acc[...] = jnp.zeros_like(acc)

    c = meta_ref[0]
    count = bc_ref[i]

    def run(slots):
        starts = [slot_rows(bl_ref, c, i, j, nb) for j in range(slots)]
        here = pl.ds(pl.multiple_of(i * BLOCK_SIZE, BLOCK_SIZE), BLOCK_SIZE)
        for g in range(CORE_KV):
            qs = wide_part(q_ref, g)
            dos = stack_heads(do_sc[s, here, g * WIDE:(g + 1) * WIDE])
            outs = wide_part(a_ref, g)
            row_dot = jnp.sum((dos.astype(F32) * outs.astype(F32)).T, axis=0, keepdims=True)
            k_cat = slot_cat(kv_sc, s, g, starts)
            v_cat = slot_cat(kv_sc, s, CORE_KV + g, starts)
            s_t = masked_scores(k_cat, qs, slots, count)
            p = jnp.exp2(s_t * EXP2_SCALE - st_ref[0, g])
            dp = lax.dot_general(v_cat, dos, NT, preferred_element_type=F32)
            ds = (p * (dp - row_dot)).astype(BF16)
            dv = dot(p.astype(BF16), dos)
            dk = dot(ds, qs) * SCALE
            dq_t = dot(k_cat.T, ds) * SCALE
            for h in range(GROUP):
                part = dq_t[:, h * BLOCK_SIZE:(h + 1) * BLOCK_SIZE]
                lane = g * WIDE + h * HEAD_DIM
                dq_ref[0, :, lane:lane + HEAD_DIM] = part.T.astype(BF16)
            lanes = slice(g * HEAD_DIM, (g + 1) * HEAD_DIM)
            for j in range(slots):
                at = pl.ds(pl.multiple_of(bl_ref[i, j] * BLOCK_SIZE, BLOCK_SIZE), BLOCK_SIZE)
                acc[0, at, lanes] += dk[j * BLOCK_SIZE:(j + 1) * BLOCK_SIZE]
                acc[1, at, lanes] += dv[j * BLOCK_SIZE:(j + 1) * BLOCK_SIZE]

    by_count(count, run)

    @pl.when(i == nb - 1)
    def _():
        dkv_ref[0] = acc[...].astype(BF16)


def backward(bl, bc, meta, q, a, st, g0, g1, kvs, plan, arrays, weight=20):
    nc, rows = len(kvs) // 2, q.shape[1]
    nb, width = rows // BLOCK_SIZE, arrays[0].shape[-1]
    wide = pl.BlockSpec((1, BLOCK_SIZE, HALF), lambda n, *_: (n // nb, n % nb, 0))
    whole = pl.BlockSpec(memory_space=pltpu.VMEM)
    return pl.pallas_call(
        functools.partial(backward_kernel, nc, nb, plan, width),
        grid_spec=pltpu.PrefetchScalarGridSpec(
            num_scalar_prefetch=3,
            grid=(2 * nb,),
            in_specs=[
                wide,
                wide,
                pl.BlockSpec((1, CORE_KV, 1, STACK), lambda n, *_: (n, 0, 0, 0)),
                whole,
                whole,
                *[whole] * (2 * nc),
                *[whole] * len(arrays),
            ],
            out_specs=[wide, pl.BlockSpec((1, 2, nc * rows, KV_HALF), lambda n, *_: (n // nb, 0, 0, 0))],
            scratch_shapes=[
                pltpu.VMEM((2, 2 * CORE_KV, nc * rows, HEAD_DIM), BF16),
                pltpu.VMEM((2, rows, HALF), BF16),
                pltpu.VMEM((2, nc * rows, KV_HALF), F32),
            ],
        ),
        out_shape=[
            jax.ShapeDtypeStruct((2, rows, HALF), BF16),
            jax.ShapeDtypeStruct((2, 2, nc * rows, KV_HALF), BF16),
        ],
        compiler_params=params(1),
        cost_estimate=cost(weight),
        name="attention_backward",
    )(bl, bc, meta, q, a, st, g0, g1, *kvs, *arrays)


def column(meta_ref, chip, core, width):
    at = ((meta_ref[2] ^ chip) * 2 + (meta_ref[1] ^ core)) * width
    return pl.ds(pl.multiple_of(at, width), width)


def read_piece(w_refs, piece):
    ref, lead, start = piece
    rows = pl.ds(start, HALF // 2)
    return w_refs[ref][rows, :] if lead is None else w_refs[ref][lead, rows, :]


def output_grad_product(plan, width, meta_ref, g_refs, w_refs):
    grads = jnp.concatenate(
        [
            jnp.concatenate([ref[:, column(meta_ref, chip, core, width)] for ref in g_refs], axis=0)
            for chip, core, _ in plan
        ],
        axis=1,
    )
    for r in range(2):
        w = jnp.concatenate([read_piece(w_refs, pieces[r]) for _, _, pieces in plan], axis=1)
        yield slice(r * (HALF // 2), (r + 1) * (HALF // 2)), lax.dot_general(
            grads, w, NT, preferred_element_type=F32
        )


def mix_kernel(plan, width, meta_ref, a_ref, resid_ref, *rest):
    w_refs, (own_ref, other_ref) = rest[:-2], rest[-2:]
    rows = resid_ref.shape[0]
    a = jnp.concatenate([a_ref[0], a_ref[1]], axis=0)
    for chip, core, pieces in plan:
        at = column(meta_ref, chip, core, width)
        part = dot(a, jnp.concatenate([read_piece(w_refs, piece) for piece in pieces], axis=0))
        own_ref[:, at] = part[:rows] + resid_ref[:, at].astype(F32)
        other_ref[:, at] = part[rows:].astype(BF16)


def mix(meta, a, resid, plan, arrays, weight=20):
    width = arrays[0].shape[-1]
    whole = pl.BlockSpec(memory_space=pltpu.VMEM)
    return pl.pallas_call(
        functools.partial(mix_kernel, plan, width),
        in_specs=[pl.BlockSpec(memory_space=pltpu.SMEM)] + [whole] * (2 + len(arrays)),
        out_specs=[whole, whole],
        out_shape=[jax.ShapeDtypeStruct(resid.shape, F32), jax.ShapeDtypeStruct(resid.shape, BF16)],
        compiler_params=params(0),
        cost_estimate=cost(weight),
        name="mix",
    )(meta, a, resid, *arrays)


def proj_kernel(count, width, cols_ref, g0_ref, g1_ref, *refs):
    inputs, outputs = refs[:8], refs[8:]
    for r in range(2):
        at_ref, far_ref, near0_ref, near1_ref = inputs[4 * r:4 * r + 4]
        lhs = jnp.concatenate([at_ref[0], at_ref[1], far_ref[0], far_ref[1]], axis=1)
        for n in range(count):
            for side in range(2):
                own = pl.ds(pl.multiple_of(cols_ref[r, n, side, 0], width), width)
                near = pl.ds(pl.multiple_of(cols_ref[r, n, side, 1], width), width)
                rhs = [g0_ref[:, own], g1_ref[:, own], near0_ref[:, near], near1_ref[:, near]]
                out = dot(lhs, jnp.concatenate(rhs, axis=0))
                outputs[(r * count + n) * 2 + side][...] = out.astype(BF16)


def proj_parts(cols, g0, g1, inputs, width, weight=20):
    count = cols.shape[1]
    whole = pl.BlockSpec(memory_space=pltpu.VMEM)
    return pl.pallas_call(
        functools.partial(proj_kernel, count, width),
        in_specs=[pl.BlockSpec(memory_space=pltpu.SMEM)] + [whole] * 10,
        out_specs=[whole] * (4 * count),
        out_shape=[jax.ShapeDtypeStruct((WIDE, width), BF16)] * (4 * count),
        compiler_params=params(0),
        cost_estimate=cost(weight),
        name="proj_parts",
    )(cols, g0, g1, *inputs)


def halve_kernel(meta_ref, q0_ref, q1_ref, out_ref):
    out_ref[0] = q0_ref[...]
    out_ref[1] = q1_ref[...]


def halve(meta, q0, q1, weight=20):
    rows = q0.shape[0]
    half = pl.BlockSpec((rows, HALF), lambda n, m: (0, m[1]))
    return pl.pallas_call(
        halve_kernel,
        grid_spec=pltpu.PrefetchScalarGridSpec(
            num_scalar_prefetch=1,
            grid=(1,),
            in_specs=[half, half],
            out_specs=pl.BlockSpec((2, rows, HALF), lambda n, m: (0, 0, 0)),
        ),
        out_shape=jax.ShapeDtypeStruct((2, rows, HALF), BF16),
        compiler_params=params(1),
        cost_estimate=cost(weight),
        name="halve",
    )(meta, q0, q1)


def after(x, *earlier):
    return lax.optimization_barrier((x, *earlier))[0]


def local(nc, nf, queries, keys, values, resid, grad_out, w_out, block_list, block_count):
    chips = nf // 2
    bits = [1 << b for b in range(chips.bit_length() - 1)]
    routes = (bits, bits[::-1])
    mid = HALF // 2
    c = lax.axis_index("ctx")
    f = lax.axis_index("fsdp")
    core, chip = f % 2, f // 2
    meta = jnp.stack([c, core, chip]).astype(jnp.int32)
    rows = queries.shape[1]
    width = w_out.shape[1]

    def to_core(x):
        return lax.ppermute(x, "fsdp", [(p, p ^ 1) for p in range(nf)])

    def to_chip(x, bit):
        return lax.ppermute(x, "fsdp", [(p, p ^ (2 * bit)) for p in range(nf)])

    def place(mine, theirs, axis):
        return jnp.where(
            core == 0,
            jnp.concatenate([mine, theirs], axis=axis),
            jnp.concatenate([theirs, mine], axis=axis),
        )

    def kv_part(which):
        cut = lambda x: lax.dynamic_slice_in_dim(x[0], which * KV_HALF, KV_HALF, 1)
        return jnp.concatenate([cut(keys), cut(values)], axis=1)

    def hop_up(x, step):
        return lax.ppermute(x, "ctx", [(p, p + 1) for p in range(step - 1, nc - 1)])

    q0, g0 = queries[0], grad_out[0]
    w_mine = lax.dynamic_slice_in_dim(w_out, core * HALF, HALF, 0)
    kvs0 = [kv_part(core)]
    kvs1 = [to_core(kv_part(1 - core))]
    w_theirs = to_core(lax.dynamic_slice_in_dim(w_out, (1 - core) * HALF, HALF, 0))

    arrays = [w_mine, w_theirs]
    held = {(0, side, r): (side, None, r * mid) for side in range(2) for r in range(2)}
    last = {}
    for side in range(2):
        for bit in bits:
            got = to_chip(after(arrays[side], *last.get(bit, ())), bit)
            for r in range(2):
                held[bit, side, r] = (len(arrays), None, r * mid)
            arrays.append(got)
            last[bit] = (got,)
    for step in range(1, nc):
        kvs0.append(hop_up(kvs0[-1], step))
        kvs1.append(hop_up(kvs1[-1], step))
    for step in range(1, len(bits)):
        for r in range(2):
            bit = routes[r][step]
            known = [0]
            for earlier in routes[r][:step]:
                known += [rel ^ earlier for rel in known]
            sources = [(rel, side) for rel in known[1:] for side in range(2)]
            parts = []
            for source in sources:
                ref, lead, first = held[(*source, r)]
                x = arrays[ref] if lead is None else arrays[ref][lead]
                parts.append(x[first:first + mid])
            got = to_chip(after(jnp.stack(parts), *last[bit], kvs0[nc - 2], kvs1[nc - 2]), bit)
            for n, (rel, side) in enumerate(sources):
                held[rel ^ bit, side, r] = (len(arrays), n, 0)
            arrays.append(got)
            last[bit] = (got,)
    w_gate = [x for bit in bits for x in last[bit]]
    g1 = to_core(after(g0, w_theirs, kvs1[0]))
    q1 = to_core(after(q0, g1))
    plan = [
        (rel, core_bit, [held[rel, core_bit, r] for r in range(2)]) for rel in range(chips) for core_bit in range(2)
    ]
    with_bit = [[rel for rel in range(chips) if rel & route[0]] for route in routes]
    without = [[rel ^ routes[r][0] for rel in with_bit[r]] for r in range(2)]

    def grad_columns(rels):
        cut = lambda rel: lax.dynamic_slice_in_dim(g0, (chip ^ rel) * 2 * width, 2 * width, 1)
        return jnp.concatenate([cut(rel) for rel in rels], axis=1)

    near_grads = []
    for r in range(2):
        bit = routes[r][0]
        near_grads.append(to_chip(after(grad_columns(with_bit[r]), *w_gate), bit))

    q_both = halve(meta, after(q0, kvs0[nc - 2], kvs1[nc - 2]), q1)
    kvs0[-1], kvs1[-1] = after(kvs0[-1], q_both), after(kvs1[-1], q_both)
    kvs = kvs0 + kvs1
    a_both, *at, st = forward(block_list, block_count, meta, q_both, kvs)
    near_grads = [(got, to_core(got)) for got in (after(got, a_both) for got in near_grads)]
    far_at = [to_chip(after(at[r], near_grads[r][0]), routes[r][0]) for r in range(2)]
    dq, dkv = backward(block_list, block_count, meta, q_both, a_both, st, g0, g1, kvs, plan, arrays)

    def total(parts):
        return functools.reduce(jnp.add, [x.astype(F32) for x in parts])

    class Chain:
        def __init__(self, shard, sign):
            self.shard, self.sign, self.step = shard, sign, 0

        def send(self):
            self.step += 1
            t = jnp.clip(c - self.sign * (self.step - nc), 0, nc - 1)
            own = self.shard(t)
            self.sent = own if self.step == 1 else total([own, self.got]).astype(BF16)
            reach = [p for p in range(nc) if (nc - 1 - p if self.sign < 0 else p) < self.step]
            pairs = [(p, p + self.sign) for p in reach if 0 <= p + self.sign < nc]
            self.got = lax.ppermute(self.sent, "ctx", pairs)

        def gate(self, *earlier):
            self.got = after(self.got, *earlier)

        def result(self):
            while self.step < nc - 1:
                self.send()
            return self.got

    kv_shard = lambda t: lax.dynamic_slice_in_dim(dkv, t * rows, rows, 2)
    kv_down = Chain(kv_shard, -1)
    kv_down.send()

    inputs = []
    for r in range(2):
        inputs += [at[r], after(far_at[r], dkv), *near_grads[r]]
    order = [
        [[jnp.stack([((chip ^ rel) * 2 + (core ^ side)) * width, (n * 2 + (core ^ side)) * width]) for side in range(2)]
         for n, rel in enumerate(without[r])]
        for r in range(2)
    ]
    cols = jnp.stack([jnp.stack([jnp.stack(pair) for pair in route]) for route in order]).astype(jnp.int32)
    parts = proj_parts(after(cols, kv_down.sent), g0, g1, inputs, width)
    count = len(without[0])
    kv_down.gate(parts[0])
    kv_down.send()
    query_grad = place(dq[0], after(to_core(dq[1]), parts[0]), 1)
    own_mix, other_mix = mix(meta, after(a_both, parts[0], kv_down.sent, query_grad), resid[0], plan, arrays)
    kv_down.gate(other_mix)
    kv_down.send()

    def reduce_chips(r):
        have = {(rel, side): parts[(r * count + n) * 2 + side] for n, rel in enumerate(without[r]) for side in range(2)}
        for bit in routes[r][1:-1]:
            far = sorted({rel for rel, _ in have if rel & bit})
            for side in range(2):
                got = to_chip(jnp.stack([have.pop((rel, side)).astype(BF16) for rel in far]), bit)
                for n, rel in enumerate(far):
                    have[rel ^ bit, side] = total([have[rel ^ bit, side], got[n]])
        bit = routes[r][-1]
        same = to_chip(have[bit, 0].astype(BF16), bit)
        cross = lax.ppermute(have[bit, 1].astype(BF16), "fsdp", [(p, p ^ (2 * bit) ^ 1) for p in range(nf)])
        return have[0, 0], have[0, 1], after(same, other_mix), after(cross, other_mix)

    reduced = [reduce_chips(r) for r in range(2)]
    swapped = to_core(after(jnp.concatenate([part[1].astype(BF16) for part in reduced], axis=0), other_mix))
    mine = [total([near, same]) for near, _, same, _ in reduced]
    theirs = [total([swapped[r * mid:(r + 1) * mid], reduced[r][3]]) for r in range(2)]
    proj_rows = jnp.concatenate(mine + theirs, axis=0).astype(BF16)
    proj_rows = after(proj_rows, kv_down.sent)
    share = QUERY_HEADS * HEAD_DIM // nc

    def proj_shard(t):
        start = t * share
        return lax.dynamic_slice_in_dim(proj_rows, start + (core * HALF) * jnp.where(start < HALF, 1, -1), share, 0)

    proj_down, proj_up = Chain(proj_shard, -1), Chain(proj_shard, 1)
    proj_grad = total([proj_shard(c), proj_down.result(), proj_up.result()])
    kv_sum = total([kv_shard(c), kv_down.result()]).astype(BF16)
    mixed = total([own_mix, to_core(other_mix)]).astype(BF16)
    grads = place(kv_sum[0], to_core(kv_sum[1]), 2)
    return mixed[None], query_grad[None], grads[:1], grads[1:], proj_grad


def solution(mesh):
    rows = P("fsdp", "ctx", None)
    body = functools.partial(local, mesh.shape["ctx"], mesh.shape["fsdp"])
    return jax.shard_map(
        body,
        mesh=mesh,
        in_specs=(rows, rows, rows, rows, rows, P(None, "fsdp"), P("ctx", None), P("ctx")),
        out_specs=(rows, rows, rows, rows, P("ctx", "fsdp")),
        check_vma=False,
    )
```

```python
import functools
import math

import jax
import jax.numpy as jnp
from jax import lax
from jax.experimental import pallas as pl
from jax.experimental.pallas import tpu as pltpu
from jax.sharding import PartitionSpec as P

QUERY_HEADS = 16
KEY_VALUE_HEADS = 4
HEAD_DIM = 128
BLOCK_SIZE = 128
KEY_SLOTS = 8

GROUP = QUERY_HEADS // KEY_VALUE_HEADS
CORE_KV = KEY_VALUE_HEADS // 2
HALF = QUERY_HEADS * HEAD_DIM // 2
KV_HALF = CORE_KV * HEAD_DIM
STACK = GROUP * BLOCK_SIZE
WIDE = GROUP * HEAD_DIM
SCALE = 1.0 / math.sqrt(HEAD_DIM)
EXP2_SCALE = SCALE * math.log2(math.e)
NEG = -1e30
F32 = jnp.float32
BF16 = jnp.bfloat16
VMEM_LIMIT = 56 * 1024 * 1024
NT = (((1,), (1,)), ((), ()))


def dot(a, b):
    return jnp.dot(a, b, preferred_element_type=F32)


def stack_heads(x):
    return jnp.concatenate([x[:, h * HEAD_DIM:(h + 1) * HEAD_DIM] for h in range(GROUP)], axis=0)


def cost(weight):
    return pl.CostEstimate(flops=int(weight * 1e9), bytes_accessed=1_000_000, transcendentals=0)


def params(steps):
    return pltpu.CompilerParams(dimension_semantics=("arbitrary",) * steps, vmem_limit_bytes=VMEM_LIMIT)


def fill_kv(kv_refs, kv_sc, rows, nc):
    for n, ref in enumerate(kv_refs):
        d = n % nc
        for u in range(2 * CORE_KV):
            kv_sc[n // nc, u, d * rows:(d + 1) * rows, :] = ref[:, u * HEAD_DIM:(u + 1) * HEAD_DIM]


def slot_rows(bl_ref, c, i, j, nb):
    b = bl_ref[i, j]
    chip = b // nb
    return pl.multiple_of(((c - chip) * nb + (b - chip * nb)) * BLOCK_SIZE, BLOCK_SIZE)


def masked_scores(k_cat, qs, slots, count):
    s_t = lax.dot_general(k_cat, qs, NT, preferred_element_type=F32)
    key = lax.broadcasted_iota(jnp.int32, (BLOCK_SIZE, STACK), 0)
    query = lax.broadcasted_iota(jnp.int32, (BLOCK_SIZE, STACK), 1) & (BLOCK_SIZE - 1)
    parts = [jnp.where(key <= query, s_t[:BLOCK_SIZE], NEG)]
    for j in range(1, slots):
        parts.append(jnp.where(j < count, s_t[j * BLOCK_SIZE:(j + 1) * BLOCK_SIZE], NEG))
    return jnp.concatenate(parts, axis=0)


def by_count(count, run):
    small = KEY_SLOTS // 2

    @pl.when(count <= small)
    def _():
        run(small)

    @pl.when(count > small)
    def _():
        run(KEY_SLOTS)


def wide_part(ref, g):
    return stack_heads(ref[0, :, g * WIDE:(g + 1) * WIDE])


def slot_cat(kv_sc, s, u, starts):
    return jnp.concatenate([kv_sc[s, u, pl.ds(at, BLOCK_SIZE), :] for at in starts], axis=0)


def forward_kernel(nc, nb, bl_ref, bc_ref, meta_ref, q_ref, *rest):
    kv_refs, (a_ref, *at_refs, st_ref, kv_sc) = rest[:2 * nc], rest[2 * nc:]
    step = pl.program_id(0)
    s, i = step // nb, step % nb

    @pl.when(step == 0)
    def _():
        fill_kv(kv_refs, kv_sc, nb * BLOCK_SIZE, nc)

    c = meta_ref[0]
    count = bc_ref[i]

    def run(slots):
        starts = [slot_rows(bl_ref, c, i, j, nb) for j in range(slots)]
        for g in range(CORE_KV):
            qs = wide_part(q_ref, g)
            k_cat = slot_cat(kv_sc, s, g, starts)
            v_cat = slot_cat(kv_sc, s, CORE_KV + g, starts)
            s_t = masked_scores(k_cat, qs, slots, count)
            top = jnp.max(s_t, axis=0, keepdims=True)
            p = jnp.exp2((s_t - top) * EXP2_SCALE)
            total = jnp.sum(p, axis=0, keepdims=True)
            a_t = dot(v_cat.T, p.astype(BF16)) / total
            st_ref[0, g] = top * EXP2_SCALE + jnp.log2(total)
            for h in range(GROUP):
                part = a_t[:, h * BLOCK_SIZE:(h + 1) * BLOCK_SIZE]
                at_refs[g][0, h * HEAD_DIM:(h + 1) * HEAD_DIM, :] = part.astype(BF16)
                lane = g * WIDE + h * HEAD_DIM
                a_ref[0, :, lane:lane + HEAD_DIM] = part.T.astype(BF16)

    by_count(count, run)


def kv_specs(nc, rows):
    return [pl.BlockSpec((rows, 2 * KV_HALF), lambda n, *_: (0, 0)) for _ in range(2 * nc)]


def forward(bl, bc, meta, q, kvs, weight=20):
    nc, rows = len(kvs) // 2, q.shape[1]
    nb = rows // BLOCK_SIZE
    wide = pl.BlockSpec((1, BLOCK_SIZE, HALF), lambda n, *_: (n // nb, n % nb, 0))
    turned = pl.BlockSpec((1, WIDE, BLOCK_SIZE), lambda n, *_: (n // nb, 0, n % nb))
    return pl.pallas_call(
        functools.partial(forward_kernel, nc, nb),
        grid_spec=pltpu.PrefetchScalarGridSpec(
            num_scalar_prefetch=3,
            grid=(2 * nb,),
            in_specs=[wide, *kv_specs(nc, rows)],
            out_specs=[wide, *[turned] * CORE_KV, pl.BlockSpec((1, CORE_KV, 1, STACK), lambda n, *_: (n, 0, 0, 0))],
            scratch_shapes=[pltpu.VMEM((2, 2 * CORE_KV, nc * rows, HEAD_DIM), BF16)],
        ),
        out_shape=[
            jax.ShapeDtypeStruct((2, rows, HALF), BF16),
            *[jax.ShapeDtypeStruct((2, WIDE, rows), BF16)] * CORE_KV,
            jax.ShapeDtypeStruct((2 * nb, CORE_KV, 1, STACK), F32),
        ],
        compiler_params=params(1),
        cost_estimate=cost(weight),
        name="attention_forward",
    )(bl, bc, meta, q, *kvs)


def backward_kernel(nc, nb, plan, width, bl_ref, bc_ref, meta_ref, q_ref, a_ref, st_ref, *rest):
    kv_refs, rest = rest[:nc], rest[nc:]
    if plan:
        (g0_ref, g1_ref, *w_refs), (dq_ref, dkv_ref, spare_ref, kv_sc, acc, do_ref) = rest[:-6], rest[-6:]
    else:
        do_ref, dq_ref, dkv_ref, kv_sc, acc = rest
    i = pl.program_id(0)
    rows = nb * BLOCK_SIZE

    @pl.when(i == 0)
    def _():
        if plan:
            for span, part in output_grad_product(plan, width, meta_ref, (g0_ref, g1_ref), w_refs):
                spare_ref[:, span] = part[:rows].astype(BF16)
                do_ref[:, span] = part[rows:].astype(BF16)
        fill_kv(kv_refs, kv_sc, rows, nc)
        acc[...] = jnp.zeros_like(acc)

    c = meta_ref[0]
    count = bc_ref[i]

    def run(slots):
        starts = [slot_rows(bl_ref, c, i, j, nb) for j in range(slots)]
        here = pl.ds(pl.multiple_of(i * BLOCK_SIZE, BLOCK_SIZE), BLOCK_SIZE)
        for g in range(CORE_KV):
            qs = wide_part(q_ref, g)
            dos = stack_heads(do_ref[here, g * WIDE:(g + 1) * WIDE])
            outs = wide_part(a_ref, g)
            row_dot = jnp.sum((dos.astype(F32) * outs.astype(F32)).T, axis=0, keepdims=True)
            k_cat = slot_cat(kv_sc, 0, g, starts)
            v_cat = slot_cat(kv_sc, 0, CORE_KV + g, starts)
            s_t = masked_scores(k_cat, qs, slots, count)
            p = jnp.exp2(s_t * EXP2_SCALE - st_ref[0, g])
            dp = lax.dot_general(v_cat, dos, NT, preferred_element_type=F32)
            ds = (p * (dp - row_dot)).astype(BF16)
            dv = dot(p.astype(BF16), dos)
            dk = dot(ds, qs) * SCALE
            dq_t = dot(k_cat.T, ds) * SCALE
            for h in range(GROUP):
                part = dq_t[:, h * BLOCK_SIZE:(h + 1) * BLOCK_SIZE]
                lane = g * WIDE + h * HEAD_DIM
                dq_ref[:, lane:lane + HEAD_DIM] = part.T.astype(BF16)
            lanes = slice(g * HEAD_DIM, (g + 1) * HEAD_DIM)
            for j in range(slots):
                at = pl.ds(pl.multiple_of(bl_ref[i, j] * BLOCK_SIZE, BLOCK_SIZE), BLOCK_SIZE)
                acc[0, at, lanes] += dk[j * BLOCK_SIZE:(j + 1) * BLOCK_SIZE]
                acc[1, at, lanes] += dv[j * BLOCK_SIZE:(j + 1) * BLOCK_SIZE]

    by_count(count, run)

    @pl.when(i == nb - 1)
    def _():
        dkv_ref[...] = acc[...].astype(BF16)


def backward(bl, bc, meta, s, q, a, st, kvs, extra, plan=(), weight=20):
    nc, rows = len(kvs), q.shape[1]
    nb, width = rows // BLOCK_SIZE, extra[-1].shape[-1]
    wide = pl.BlockSpec((1, BLOCK_SIZE, HALF), lambda n, *_: (s, n, 0))
    whole = pl.BlockSpec(memory_space=pltpu.VMEM)
    grad = jax.ShapeDtypeStruct((rows, HALF), BF16)
    return pl.pallas_call(
        functools.partial(backward_kernel, nc, nb, plan, width),
        grid_spec=pltpu.PrefetchScalarGridSpec(
            num_scalar_prefetch=3,
            grid=(nb,),
            in_specs=[
                wide,
                wide,
                pl.BlockSpec((1, CORE_KV, 1, STACK), lambda n, *_: (s * nb + n, 0, 0, 0)),
                *[whole] * (nc + len(extra)),
            ],
            out_specs=[
                pl.BlockSpec((BLOCK_SIZE, HALF), lambda n, *_: (n, 0)),
                pl.BlockSpec((2, nc * rows, KV_HALF), lambda n, *_: (0, 0, 0)),
                *[pl.BlockSpec((rows, HALF), lambda n, *_: (0, 0))] * bool(plan),
            ],
            scratch_shapes=[
                pltpu.VMEM((1, 2 * CORE_KV, nc * rows, HEAD_DIM), BF16),
                pltpu.VMEM((2, nc * rows, KV_HALF), F32),
                *[pltpu.VMEM((rows, HALF), BF16)] * bool(plan),
            ],
        ),
        out_shape=[grad, jax.ShapeDtypeStruct((2, nc * rows, KV_HALF), BF16), *[grad] * bool(plan)],
        compiler_params=params(1),
        cost_estimate=cost(weight),
        name="attention_backward",
    )(bl, bc, meta, q, a, st, *kvs, *extra)


def column(meta_ref, chip, core, width):
    at = ((meta_ref[2] ^ chip) * 2 + (meta_ref[1] ^ core)) * width
    return pl.ds(pl.multiple_of(at, width), width)


def read_piece(w_refs, piece):
    ref, lead, start = piece
    rows = pl.ds(start, HALF // 2)
    return w_refs[ref][rows, :] if lead is None else w_refs[ref][lead, rows, :]


def output_grad_product(plan, width, meta_ref, g_refs, w_refs):
    grads = jnp.concatenate(
        [
            jnp.concatenate([ref[:, column(meta_ref, chip, core, width)] for ref in g_refs], axis=0)
            for chip, core, _ in plan
        ],
        axis=1,
    )
    for r in range(2):
        w = jnp.concatenate([read_piece(w_refs, pieces[r]) for _, _, pieces in plan], axis=1)
        yield slice(r * (HALF // 2), (r + 1) * (HALF // 2)), lax.dot_general(
            grads, w, NT, preferred_element_type=F32
        )


def mix_kernel(plan, width, meta_ref, a_ref, resid_ref, *rest):
    w_refs, (own_ref, other_ref) = rest[:-2], rest[-2:]
    rows = resid_ref.shape[0]
    a = jnp.concatenate([a_ref[0], a_ref[1]], axis=0)
    for chip, core, pieces in plan:
        at = column(meta_ref, chip, core, width)
        part = dot(a, jnp.concatenate([read_piece(w_refs, piece) for piece in pieces], axis=0))
        own_ref[:, at] = part[:rows] + resid_ref[:, at].astype(F32)
        other_ref[:, at] = part[rows:].astype(BF16)


def mix(meta, a, resid, plan, arrays, weight=20):
    width = arrays[0].shape[-1]
    whole = pl.BlockSpec(memory_space=pltpu.VMEM)
    return pl.pallas_call(
        functools.partial(mix_kernel, plan, width),
        in_specs=[pl.BlockSpec(memory_space=pltpu.SMEM)] + [whole] * (2 + len(arrays)),
        out_specs=[whole, whole],
        out_shape=[jax.ShapeDtypeStruct(resid.shape, F32), jax.ShapeDtypeStruct(resid.shape, BF16)],
        compiler_params=params(0),
        cost_estimate=cost(weight),
        name="mix",
    )(meta, a, resid, *arrays)


def proj_kernel(count, width, cols_ref, g0_ref, g1_ref, *refs):
    inputs, outputs = refs[:8], refs[8:]
    for r in range(2):
        at_ref, far_ref, near0_ref, near1_ref = inputs[4 * r:4 * r + 4]
        lhs = jnp.concatenate([at_ref[0], at_ref[1], far_ref[0], far_ref[1]], axis=1)
        for n in range(count):
            for side in range(2):
                own = pl.ds(pl.multiple_of(cols_ref[r, n, side, 0], width), width)
                near = pl.ds(pl.multiple_of(cols_ref[r, n, side, 1], width), width)
                rhs = [g0_ref[:, own], g1_ref[:, own], near0_ref[:, near], near1_ref[:, near]]
                out = dot(lhs, jnp.concatenate(rhs, axis=0))
                outputs[(r * count + n) * 2 + side][...] = out.astype(BF16)


def proj_parts(cols, g0, g1, inputs, width, weight=20):
    count = cols.shape[1]
    whole = pl.BlockSpec(memory_space=pltpu.VMEM)
    return pl.pallas_call(
        functools.partial(proj_kernel, count, width),
        in_specs=[pl.BlockSpec(memory_space=pltpu.SMEM)] + [whole] * 10,
        out_specs=[whole] * (4 * count),
        out_shape=[jax.ShapeDtypeStruct((WIDE, width), BF16)] * (4 * count),
        compiler_params=params(0),
        cost_estimate=cost(weight),
        name="proj_parts",
    )(cols, g0, g1, *inputs)


def halve_kernel(meta_ref, q0_ref, q1_ref, out_ref):
    out_ref[0] = q0_ref[...]
    out_ref[1] = q1_ref[...]


def halve(meta, q0, q1, weight=20):
    rows = q0.shape[0]
    half = pl.BlockSpec((rows, HALF), lambda n, m: (0, m[1]))
    return pl.pallas_call(
        halve_kernel,
        grid_spec=pltpu.PrefetchScalarGridSpec(
            num_scalar_prefetch=1,
            grid=(1,),
            in_specs=[half, half],
            out_specs=pl.BlockSpec((2, rows, HALF), lambda n, m: (0, 0, 0)),
        ),
        out_shape=jax.ShapeDtypeStruct((2, rows, HALF), BF16),
        compiler_params=params(1),
        cost_estimate=cost(weight),
        name="halve",
    )(meta, q0, q1)


def after(x, *earlier):
    return lax.optimization_barrier((x, *earlier))[0]


def local(nc, nf, queries, keys, values, resid, grad_out, w_out, block_list, block_count):
    chips = nf // 2
    bits = [1 << b for b in range(chips.bit_length() - 1)]
    routes = (bits, bits[::-1])
    mid = HALF // 2
    c = lax.axis_index("ctx")
    f = lax.axis_index("fsdp")
    core, chip = f % 2, f // 2
    meta = jnp.stack([c, core, chip]).astype(jnp.int32)
    rows = queries.shape[1]
    width = w_out.shape[1]

    def to_core(x):
        return lax.ppermute(x, "fsdp", [(p, p ^ 1) for p in range(nf)])

    def to_chip(x, bit):
        return lax.ppermute(x, "fsdp", [(p, p ^ (2 * bit)) for p in range(nf)])

    def place(mine, theirs, axis):
        return jnp.where(
            core == 0,
            jnp.concatenate([mine, theirs], axis=axis),
            jnp.concatenate([theirs, mine], axis=axis),
        )

    def kv_part(which):
        cut = lambda x: lax.dynamic_slice_in_dim(x[0], which * KV_HALF, KV_HALF, 1)
        return jnp.concatenate([cut(keys), cut(values)], axis=1)

    def hop_up(x, step):
        return lax.ppermute(x, "ctx", [(p, p + 1) for p in range(step - 1, nc - 1)])

    q0, g0 = queries[0], grad_out[0]
    w_mine = lax.dynamic_slice_in_dim(w_out, core * HALF, HALF, 0)
    kvs0 = [kv_part(core)]
    kvs1 = [to_core(kv_part(1 - core))]
    w_theirs = to_core(lax.dynamic_slice_in_dim(w_out, (1 - core) * HALF, HALF, 0))

    arrays = [w_mine, w_theirs]
    held = {(0, side, r): (side, None, r * mid) for side in range(2) for r in range(2)}
    last = {}
    for side in range(2):
        for bit in bits:
            got = to_chip(after(arrays[side], *last.get(bit, ())), bit)
            for r in range(2):
                held[bit, side, r] = (len(arrays), None, r * mid)
            arrays.append(got)
            last[bit] = (got,)
    for step in range(1, nc):
        kvs0.append(hop_up(kvs0[-1], step))
        kvs1.append(hop_up(kvs1[-1], step))
    for step in range(1, len(bits)):
        for r in range(2):
            bit = routes[r][step]
            known = [0]
            for earlier in routes[r][:step]:
                known += [rel ^ earlier for rel in known]
            sources = [(rel, side) for rel in known[1:] for side in range(2)]
            parts = []
            for source in sources:
                ref, lead, first = held[(*source, r)]
                x = arrays[ref] if lead is None else arrays[ref][lead]
                parts.append(x[first:first + mid])
            got = to_chip(after(jnp.stack(parts), *last[bit], kvs0[nc - 2], kvs1[nc - 2]), bit)
            for n, (rel, side) in enumerate(sources):
                held[rel ^ bit, side, r] = (len(arrays), n, 0)
            arrays.append(got)
            last[bit] = (got,)
    w_gate = [x for bit in bits for x in last[bit]]
    g1 = to_core(after(g0, w_theirs, kvs1[0]))
    q1 = to_core(after(q0, g1))
    plan = [
        (rel, core_bit, [held[rel, core_bit, r] for r in range(2)]) for rel in range(chips) for core_bit in range(2)
    ]
    with_bit = [[rel for rel in range(chips) if rel & route[0]] for route in routes]
    without = [[rel ^ routes[r][0] for rel in with_bit[r]] for r in range(2)]

    def grad_columns(rels):
        cut = lambda rel: lax.dynamic_slice_in_dim(g0, (chip ^ rel) * 2 * width, 2 * width, 1)
        return jnp.concatenate([cut(rel) for rel in rels], axis=1)

    q_both = halve(meta, after(q0, kvs0[nc - 2], kvs1[nc - 2]), q1)
    kvs0[-1], kvs1[-1] = after(kvs0[-1], q_both), after(kvs1[-1], q_both)
    kvs = kvs0 + kvs1
    a_both, *at, st = forward(block_list, block_count, meta, q_both, kvs)
    near_grads = []
    for r in range(2):
        got = to_chip(after(grad_columns(with_bit[r]), *w_gate, a_both), routes[r][0])
        near_grads.append((got, to_core(got)))
    far_at = [to_chip(after(at[r], near_grads[r][0]), routes[r][0]) for r in range(2)]
    def total(parts):
        return functools.reduce(jnp.add, [x.astype(F32) for x in parts])

    class Chain:
        def __init__(self, shard, sign):
            self.shard, self.sign, self.step = shard, sign, 0

        def send(self):
            self.step += 1
            t = jnp.clip(c - self.sign * (self.step - nc), 0, nc - 1)
            own = self.shard(t)
            self.sent = own if self.step == 1 else total([own, self.got]).astype(BF16)
            reach = [p for p in range(nc) if (nc - 1 - p if self.sign < 0 else p) < self.step]
            pairs = [(p, p + self.sign) for p in reach if 0 <= p + self.sign < nc]
            self.got = lax.ppermute(self.sent, "ctx", pairs)

        def gate(self, *earlier):
            self.got = after(self.got, *earlier)

        def result(self):
            while self.step < nc - 1:
                self.send()
            return self.got

    kv_shard = lambda dkv: lambda t: lax.dynamic_slice_in_dim(dkv, t * rows, rows, 1)
    listed = (block_list, block_count, meta)
    dq1, dkv1, do0 = backward(*listed, 1, q_both, a_both, st, kvs1, (g0, g1, *arrays), plan)

    def hop_down(step, got):
        parts = []
        for lane, dkv in ((0, dkv1), (1, dkv0)):
            hop = step - lane
            if 1 <= hop < nc:
                own = kv_shard(dkv)(jnp.maximum(c + hop - nc, 0))
                parts.append(own if hop == 1 else total([own, got[lane]]).astype(BF16))
            else:
                parts.append(None)
        sending = jnp.stack([x for x in parts if x is not None])
        moved = lax.ppermute(sending, "ctx", [(p, p - 1) for p in range(max(nc - step, 1), nc)])
        return sending, moved

    def unpack(step, moved):
        return (moved[0] if step < nc else None, moved[-1] if step > 1 else None)

    dkv0 = None
    sending, moved = hop_down(1, None)
    dq0, dkv0 = backward(*listed, 0, after(q_both, sending), a_both, st, kvs0, (do0,))
    sending, moved = hop_down(2, unpack(1, after(moved, dkv0)))

    inputs = []
    for r in range(2):
        inputs += [at[r], after(far_at[r], dkv0), *near_grads[r]]
    order = [
        [[jnp.stack([((chip ^ rel) * 2 + (core ^ side)) * width, (n * 2 + (core ^ side)) * width]) for side in range(2)]
         for n, rel in enumerate(without[r])]
        for r in range(2)
    ]
    cols = jnp.stack([jnp.stack([jnp.stack(pair) for pair in route]) for route in order]).astype(jnp.int32)
    parts = proj_parts(after(cols, sending), g0, g1, inputs, width)
    count = len(without[0])
    sending, moved = hop_down(3, unpack(2, after(moved, parts[0])))
    query_grad = place(dq0, after(to_core(dq1), parts[0]), 1)[None]
    a_late, query_grad, *_ = lax.optimization_barrier((a_both, query_grad, parts[0], sending))
    own_mix, other_mix = mix(meta, a_late, resid[0], plan, arrays)
    moved = after(moved, other_mix)
    for step in range(4, nc + 1):
        if step == nc:
            sum1 = total([kv_shard(dkv1)(c), moved[0]]).astype(BF16)
        sending, moved = hop_down(step, unpack(step - 1, moved))
    sum0 = total([kv_shard(dkv0)(c), moved[-1]]).astype(BF16)

    def reduce_chips(r):
        have = {(rel, side): parts[(r * count + n) * 2 + side] for n, rel in enumerate(without[r]) for side in range(2)}
        for bit in routes[r][1:-1]:
            far = sorted({rel for rel, _ in have if rel & bit})
            for side in range(2):
                got = to_chip(jnp.stack([have.pop((rel, side)).astype(BF16) for rel in far]), bit)
                for n, rel in enumerate(far):
                    have[rel ^ bit, side] = total([have[rel ^ bit, side], got[n]])
        bit = routes[r][-1]
        same = to_chip(have[bit, 0].astype(BF16), bit)
        cross = lax.ppermute(have[bit, 1].astype(BF16), "fsdp", [(p, p ^ (2 * bit) ^ 1) for p in range(nf)])
        return have[0, 0], have[0, 1], after(same, other_mix), after(cross, other_mix)

    reduced = [reduce_chips(r) for r in range(2)]
    swapped = to_core(after(jnp.concatenate([part[1].astype(BF16) for part in reduced], axis=0), other_mix))
    mine = [total([near, same]) for near, _, same, _ in reduced]
    theirs = [total([swapped[r * mid:(r + 1) * mid], reduced[r][3]]) for r in range(2)]
    proj_rows = jnp.concatenate(mine + theirs, axis=0).astype(BF16)
    proj_rows = after(proj_rows, sending)
    share = QUERY_HEADS * HEAD_DIM // nc

    def proj_shard(t):
        start = t * share
        return lax.dynamic_slice_in_dim(proj_rows, start + (core * HALF) * jnp.where(start < HALF, 1, -1), share, 0)

    proj_down, proj_up = Chain(proj_shard, -1), Chain(proj_shard, 1)
    for _ in range(nc - 1):
        proj_down.send()
        proj_up.send()
        proj_down.got, proj_up.got = lax.optimization_barrier((proj_down.got, proj_up.got))
    proj_grad = total([proj_shard(c), proj_down.got, proj_up.got])
    mixed = total([own_mix, to_core(other_mix)]).astype(BF16)
    grads = place(sum0, to_core(sum1), 2)
    return mixed[None], query_grad, grads[:1], grads[1:], proj_grad


def solution(mesh):
    rows = P("fsdp", "ctx", None)
    body = functools.partial(local, mesh.shape["ctx"], mesh.shape["fsdp"])
    return jax.shard_map(
        body,
        mesh=mesh,
        in_specs=(rows, rows, rows, rows, rows, P(None, "fsdp"), P("ctx", None), P("ctx")),
        out_specs=(rows, rows, rows, rows, P("ctx", "fsdp")),
        check_vma=False,
    )
```

```python
import functools
import math

import jax
import jax.numpy as jnp
from jax import lax
from jax.experimental import pallas as pl
from jax.experimental.pallas import tpu as pltpu
from jax.sharding import PartitionSpec as P

QUERY_HEADS = 16
KEY_VALUE_HEADS = 4
HEAD_DIM = 128
BLOCK_SIZE = 128
KEY_SLOTS = 8

GROUP = QUERY_HEADS // KEY_VALUE_HEADS
CORE_KV = KEY_VALUE_HEADS // 2
HALF = QUERY_HEADS * HEAD_DIM // 2
KV_HALF = CORE_KV * HEAD_DIM
STACK = GROUP * BLOCK_SIZE
WIDE = GROUP * HEAD_DIM
SCALE = 1.0 / math.sqrt(HEAD_DIM)
EXP2_SCALE = SCALE * math.log2(math.e)
NEG = -1e30
F32 = jnp.float32
BF16 = jnp.bfloat16
VMEM_LIMIT = 56 * 1024 * 1024
NT = (((1,), (1,)), ((), ()))


def dot(a, b):
    return jnp.dot(a, b, preferred_element_type=F32)


def stack_heads(x):
    return jnp.concatenate([x[:, h * HEAD_DIM:(h + 1) * HEAD_DIM] for h in range(GROUP)], axis=0)


def cost(weight):
    return pl.CostEstimate(flops=int(weight * 1e9), bytes_accessed=1_000_000, transcendentals=0)


def params(steps):
    return pltpu.CompilerParams(dimension_semantics=("arbitrary",) * steps, vmem_limit_bytes=VMEM_LIMIT)


def fill_kv(kv_refs, kv_sc, rows, nc):
    for n, ref in enumerate(kv_refs):
        d = n % nc
        for u in range(2 * CORE_KV):
            kv_sc[n // nc, u, d * rows:(d + 1) * rows, :] = ref[:, u * HEAD_DIM:(u + 1) * HEAD_DIM]


def slot_rows(bl_ref, c, i, j, nb):
    b = bl_ref[i, j]
    chip = b // nb
    return pl.multiple_of(((c - chip) * nb + (b - chip * nb)) * BLOCK_SIZE, BLOCK_SIZE)


def masked_scores(k_cat, qs, slots, count):
    s_t = lax.dot_general(k_cat, qs, NT, preferred_element_type=F32)
    key = lax.broadcasted_iota(jnp.int32, (BLOCK_SIZE, STACK), 0)
    query = lax.broadcasted_iota(jnp.int32, (BLOCK_SIZE, STACK), 1) & (BLOCK_SIZE - 1)
    parts = [jnp.where(key <= query, s_t[:BLOCK_SIZE], NEG)]
    for j in range(1, slots):
        parts.append(jnp.where(j < count, s_t[j * BLOCK_SIZE:(j + 1) * BLOCK_SIZE], NEG))
    return jnp.concatenate(parts, axis=0)


def by_count(count, run):
    small = KEY_SLOTS // 2

    @pl.when(count <= small)
    def _():
        run(small)

    @pl.when(count > small)
    def _():
        run(KEY_SLOTS)


def wide_part(ref, g):
    return stack_heads(ref[0, :, g * WIDE:(g + 1) * WIDE])


def slot_cat(kv_sc, s, u, starts):
    return jnp.concatenate([kv_sc[s, u, pl.ds(at, BLOCK_SIZE), :] for at in starts], axis=0)


def forward_kernel(nc, nb, bl_ref, bc_ref, meta_ref, q_ref, *rest):
    kv_refs, (a_ref, *at_refs, st_ref, kv_sc) = rest[:2 * nc], rest[2 * nc:]
    step = pl.program_id(0)
    s, i = step // nb, step % nb

    @pl.when(step == 0)
    def _():
        fill_kv(kv_refs, kv_sc, nb * BLOCK_SIZE, nc)

    c = meta_ref[0]
    count = bc_ref[i]

    def run(slots):
        starts = [slot_rows(bl_ref, c, i, j, nb) for j in range(slots)]
        for g in range(CORE_KV):
            qs = wide_part(q_ref, g)
            k_cat = slot_cat(kv_sc, s, g, starts)
            v_cat = slot_cat(kv_sc, s, CORE_KV + g, starts)
            s_t = masked_scores(k_cat, qs, slots, count)
            top = jnp.max(s_t, axis=0, keepdims=True)
            p = jnp.exp2((s_t - top) * EXP2_SCALE)
            total = jnp.sum(p, axis=0, keepdims=True)
            a_t = dot(v_cat.T, p.astype(BF16)) / total
            st_ref[0, g] = top * EXP2_SCALE + jnp.log2(total)
            for h in range(GROUP):
                part = a_t[:, h * BLOCK_SIZE:(h + 1) * BLOCK_SIZE]
                at_refs[g][0, h * HEAD_DIM:(h + 1) * HEAD_DIM, :] = part.astype(BF16)
                lane = g * WIDE + h * HEAD_DIM
                a_ref[0, :, lane:lane + HEAD_DIM] = part.T.astype(BF16)

    by_count(count, run)


def kv_specs(nc, rows):
    return [pl.BlockSpec((rows, 2 * KV_HALF), lambda n, *_: (0, 0)) for _ in range(2 * nc)]


def forward(bl, bc, meta, q, kvs, weight=20):
    nc, rows = len(kvs) // 2, q.shape[1]
    nb = rows // BLOCK_SIZE
    wide = pl.BlockSpec((1, BLOCK_SIZE, HALF), lambda n, *_: (n // nb, n % nb, 0))
    turned = pl.BlockSpec((1, WIDE, BLOCK_SIZE), lambda n, *_: (n // nb, 0, n % nb))
    return pl.pallas_call(
        functools.partial(forward_kernel, nc, nb),
        grid_spec=pltpu.PrefetchScalarGridSpec(
            num_scalar_prefetch=3,
            grid=(2 * nb,),
            in_specs=[wide, *kv_specs(nc, rows)],
            out_specs=[wide, *[turned] * CORE_KV, pl.BlockSpec((1, CORE_KV, 1, STACK), lambda n, *_: (n, 0, 0, 0))],
            scratch_shapes=[pltpu.VMEM((2, 2 * CORE_KV, nc * rows, HEAD_DIM), BF16)],
        ),
        out_shape=[
            jax.ShapeDtypeStruct((2, rows, HALF), BF16),
            *[jax.ShapeDtypeStruct((2, WIDE, rows), BF16)] * CORE_KV,
            jax.ShapeDtypeStruct((2 * nb, CORE_KV, 1, STACK), F32),
        ],
        compiler_params=params(1),
        cost_estimate=cost(weight),
        name="attention_forward",
    )(bl, bc, meta, q, *kvs)


def backward_kernel(nc, nb, plan, width, bl_ref, bc_ref, meta_ref, q_ref, a_ref, st_ref, *rest):
    kv_refs, rest = rest[:nc], rest[nc:]
    if plan:
        (g0_ref, g1_ref, *w_refs), (dq_ref, dkv_ref, spare_ref, kv_sc, acc, do_ref) = rest[:-6], rest[-6:]
    else:
        do_ref, dq_ref, dkv_ref, kv_sc, acc = rest
    i = pl.program_id(0)
    rows = nb * BLOCK_SIZE

    @pl.when(i == 0)
    def _():
        if plan:
            for span, part in output_grad_product(plan, width, meta_ref, (g0_ref, g1_ref), w_refs):
                spare_ref[:, span] = part[:rows].astype(BF16)
                do_ref[:, span] = part[rows:].astype(BF16)
        fill_kv(kv_refs, kv_sc, rows, nc)
        acc[...] = jnp.zeros_like(acc)

    c = meta_ref[0]
    count = bc_ref[i]

    def run(slots):
        starts = [slot_rows(bl_ref, c, i, j, nb) for j in range(slots)]
        here = pl.ds(pl.multiple_of(i * BLOCK_SIZE, BLOCK_SIZE), BLOCK_SIZE)
        for g in range(CORE_KV):
            qs = wide_part(q_ref, g)
            dos = stack_heads(do_ref[here, g * WIDE:(g + 1) * WIDE])
            outs = wide_part(a_ref, g)
            row_dot = jnp.sum((dos.astype(F32) * outs.astype(F32)).T, axis=0, keepdims=True)
            k_cat = slot_cat(kv_sc, 0, g, starts)
            v_cat = slot_cat(kv_sc, 0, CORE_KV + g, starts)
            s_t = masked_scores(k_cat, qs, slots, count)
            p = jnp.exp2(s_t * EXP2_SCALE - st_ref[0, g])
            dp = lax.dot_general(v_cat, dos, NT, preferred_element_type=F32)
            ds = (p * (dp - row_dot)).astype(BF16)
            dv = dot(p.astype(BF16), dos)
            dk = dot(ds, qs) * SCALE
            dq_t = dot(k_cat.T, ds) * SCALE
            for h in range(GROUP):
                part = dq_t[:, h * BLOCK_SIZE:(h + 1) * BLOCK_SIZE]
                lane = g * WIDE + h * HEAD_DIM
                dq_ref[:, lane:lane + HEAD_DIM] = part.T.astype(BF16)
            lanes = slice(g * HEAD_DIM, (g + 1) * HEAD_DIM)
            for j in range(slots):
                at = pl.ds(pl.multiple_of(bl_ref[i, j] * BLOCK_SIZE, BLOCK_SIZE), BLOCK_SIZE)
                acc[0, at, lanes] += dk[j * BLOCK_SIZE:(j + 1) * BLOCK_SIZE]
                acc[1, at, lanes] += dv[j * BLOCK_SIZE:(j + 1) * BLOCK_SIZE]

    by_count(count, run)

    @pl.when(i == nb - 1)
    def _():
        dkv_ref[...] = acc[...].astype(BF16)


def backward(bl, bc, meta, s, q, a, st, kvs, extra, plan=(), weight=20):
    nc, rows = len(kvs), q.shape[1]
    nb, width = rows // BLOCK_SIZE, extra[-1].shape[-1]
    wide = pl.BlockSpec((1, BLOCK_SIZE, HALF), lambda n, *_: (s, n, 0))
    whole = pl.BlockSpec(memory_space=pltpu.VMEM)
    grad = jax.ShapeDtypeStruct((rows, HALF), BF16)
    return pl.pallas_call(
        functools.partial(backward_kernel, nc, nb, plan, width),
        grid_spec=pltpu.PrefetchScalarGridSpec(
            num_scalar_prefetch=3,
            grid=(nb,),
            in_specs=[
                wide,
                wide,
                pl.BlockSpec((1, CORE_KV, 1, STACK), lambda n, *_: (s * nb + n, 0, 0, 0)),
                *[whole] * (nc + len(extra)),
            ],
            out_specs=[
                pl.BlockSpec((BLOCK_SIZE, HALF), lambda n, *_: (n, 0)),
                pl.BlockSpec((2, nc * rows, KV_HALF), lambda n, *_: (0, 0, 0)),
                *[pl.BlockSpec((rows, HALF), lambda n, *_: (0, 0))] * bool(plan),
            ],
            scratch_shapes=[
                pltpu.VMEM((1, 2 * CORE_KV, nc * rows, HEAD_DIM), BF16),
                pltpu.VMEM((2, nc * rows, KV_HALF), F32),
                *[pltpu.VMEM((rows, HALF), BF16)] * bool(plan),
            ],
        ),
        out_shape=[grad, jax.ShapeDtypeStruct((2, nc * rows, KV_HALF), BF16), *[grad] * bool(plan)],
        compiler_params=params(1),
        cost_estimate=cost(weight),
        name="attention_backward",
    )(bl, bc, meta, q, a, st, *kvs, *extra)


def column(meta_ref, chip, core, width):
    at = ((meta_ref[2] ^ chip) * 2 + (meta_ref[1] ^ core)) * width
    return pl.ds(pl.multiple_of(at, width), width)


def read_piece(w_refs, piece):
    ref, lead, start = piece
    rows = pl.ds(start, HALF // 2)
    return w_refs[ref][rows, :] if lead is None else w_refs[ref][lead, rows, :]


def output_grad_product(plan, width, meta_ref, g_refs, w_refs):
    grads = jnp.concatenate(
        [
            jnp.concatenate([ref[:, column(meta_ref, chip, core, width)] for ref in g_refs], axis=0)
            for chip, core, _ in plan
        ],
        axis=1,
    )
    for r in range(2):
        w = jnp.concatenate([read_piece(w_refs, pieces[r]) for _, _, pieces in plan], axis=1)
        yield slice(r * (HALF // 2), (r + 1) * (HALF // 2)), lax.dot_general(
            grads, w, NT, preferred_element_type=F32
        )


def mix_kernel(plan, width, meta_ref, a_ref, resid_ref, *rest):
    w_refs, (own_ref, other_ref) = rest[:-2], rest[-2:]
    rows = resid_ref.shape[0]
    a = jnp.concatenate([a_ref[0], a_ref[1]], axis=0)
    for chip, core, pieces in plan:
        at = column(meta_ref, chip, core, width)
        part = dot(a, jnp.concatenate([read_piece(w_refs, piece) for piece in pieces], axis=0))
        own_ref[:, at] = part[:rows] + resid_ref[:, at].astype(F32)
        other_ref[:, at] = part[rows:].astype(BF16)


def mix(meta, a, resid, plan, arrays, weight=20):
    width = arrays[0].shape[-1]
    whole = pl.BlockSpec(memory_space=pltpu.VMEM)
    return pl.pallas_call(
        functools.partial(mix_kernel, plan, width),
        in_specs=[pl.BlockSpec(memory_space=pltpu.SMEM)] + [whole] * (2 + len(arrays)),
        out_specs=[whole, whole],
        out_shape=[jax.ShapeDtypeStruct(resid.shape, F32), jax.ShapeDtypeStruct(resid.shape, BF16)],
        compiler_params=params(0),
        cost_estimate=cost(weight),
        name="mix",
    )(meta, a, resid, *arrays)


def proj_kernel(count, width, cols_ref, g0_ref, g1_ref, *refs):
    inputs, outputs = refs[:8], refs[8:]
    for r in range(2):
        at_ref, far_ref, near0_ref, near1_ref = inputs[4 * r:4 * r + 4]
        lhs = jnp.concatenate([at_ref[0], at_ref[1], far_ref[0], far_ref[1]], axis=1)
        for n in range(count):
            for side in range(2):
                own = pl.ds(pl.multiple_of(cols_ref[r, n, side, 0], width), width)
                near = pl.ds(pl.multiple_of(cols_ref[r, n, side, 1], width), width)
                rhs = [g0_ref[:, own], g1_ref[:, own], near0_ref[:, near], near1_ref[:, near]]
                out = dot(lhs, jnp.concatenate(rhs, axis=0))
                outputs[(r * count + n) * 2 + side][...] = out.astype(BF16)


def proj_parts(cols, g0, g1, inputs, width, weight=20):
    count = cols.shape[1]
    whole = pl.BlockSpec(memory_space=pltpu.VMEM)
    return pl.pallas_call(
        functools.partial(proj_kernel, count, width),
        in_specs=[pl.BlockSpec(memory_space=pltpu.SMEM)] + [whole] * 10,
        out_specs=[whole] * (4 * count),
        out_shape=[jax.ShapeDtypeStruct((WIDE, width), BF16)] * (4 * count),
        compiler_params=params(0),
        cost_estimate=cost(weight),
        name="proj_parts",
    )(cols, g0, g1, *inputs)


def halve_kernel(meta_ref, q0_ref, q1_ref, out_ref):
    out_ref[0] = q0_ref[...]
    out_ref[1] = q1_ref[...]


def halve(meta, q0, q1, weight=20):
    rows = q0.shape[0]
    half = pl.BlockSpec((rows, HALF), lambda n, m: (0, m[1]))
    return pl.pallas_call(
        halve_kernel,
        grid_spec=pltpu.PrefetchScalarGridSpec(
            num_scalar_prefetch=1,
            grid=(1,),
            in_specs=[half, half],
            out_specs=pl.BlockSpec((2, rows, HALF), lambda n, m: (0, 0, 0)),
        ),
        out_shape=jax.ShapeDtypeStruct((2, rows, HALF), BF16),
        compiler_params=params(1),
        cost_estimate=cost(weight),
        name="halve",
    )(meta, q0, q1)


def after(x, *earlier):
    return lax.optimization_barrier((x, *earlier))[0]


def local(nc, nf, queries, keys, values, resid, grad_out, w_out, block_list, block_count):
    chips = nf // 2
    bits = [1 << b for b in range(chips.bit_length() - 1)]
    routes = (bits, bits[::-1])
    mid = HALF // 2
    c = lax.axis_index("ctx")
    f = lax.axis_index("fsdp")
    core, chip = f % 2, f // 2
    meta = jnp.stack([c, core, chip]).astype(jnp.int32)
    rows = queries.shape[1]
    width = w_out.shape[1]

    def to_core(x):
        return lax.ppermute(x, "fsdp", [(p, p ^ 1) for p in range(nf)])

    def to_chip(x, bit):
        return lax.ppermute(x, "fsdp", [(p, p ^ (2 * bit)) for p in range(nf)])

    def place(mine, theirs, axis):
        return jnp.where(
            core == 0,
            jnp.concatenate([mine, theirs], axis=axis),
            jnp.concatenate([theirs, mine], axis=axis),
        )

    def kv_part(which):
        cut = lambda x: lax.dynamic_slice_in_dim(x[0], which * KV_HALF, KV_HALF, 1)
        return jnp.concatenate([cut(keys), cut(values)], axis=1)

    def hop_up(x, step):
        return lax.ppermute(x, "ctx", [(p, p + 1) for p in range(step - 1, nc - 1)])

    q0, g0 = queries[0], grad_out[0]
    w_mine = lax.dynamic_slice_in_dim(w_out, core * HALF, HALF, 0)
    kvs0 = [kv_part(core)]
    kvs1 = [to_core(kv_part(1 - core))]
    w_theirs = to_core(lax.dynamic_slice_in_dim(w_out, (1 - core) * HALF, HALF, 0))

    arrays = [w_mine, w_theirs]
    held = {(0, side, r): (side, None, r * mid) for side in range(2) for r in range(2)}
    last = {}
    for side in range(2):
        for bit in bits:
            got = to_chip(after(arrays[side], *last.get(bit, ())), bit)
            for r in range(2):
                held[bit, side, r] = (len(arrays), None, r * mid)
            arrays.append(got)
            last[bit] = (got,)
    for step in range(1, nc):
        kvs0.append(hop_up(kvs0[-1], step))
        kvs1.append(hop_up(kvs1[-1], step))
    for step in range(1, len(bits)):
        for r in range(2):
            bit = routes[r][step]
            known = [0]
            for earlier in routes[r][:step]:
                known += [rel ^ earlier for rel in known]
            sources = [(rel, side) for rel in known[1:] for side in range(2)]
            parts = []
            for source in sources:
                ref, lead, first = held[(*source, r)]
                x = arrays[ref] if lead is None else arrays[ref][lead]
                parts.append(x[first:first + mid])
            got = to_chip(after(jnp.stack(parts), *last[bit], kvs0[nc - 2], kvs1[nc - 2]), bit)
            for n, (rel, side) in enumerate(sources):
                held[rel ^ bit, side, r] = (len(arrays), n, 0)
            arrays.append(got)
            last[bit] = (got,)
    w_gate = [x for bit in bits for x in last[bit]]
    g1 = to_core(after(g0, w_theirs, kvs1[0]))
    q1 = to_core(after(q0, g1))
    plan = [
        (rel, core_bit, [held[rel, core_bit, r] for r in range(2)]) for rel in range(chips) for core_bit in range(2)
    ]
    with_bit = [[rel for rel in range(chips) if rel & route[0]] for route in routes]
    without = [[rel ^ routes[r][0] for rel in with_bit[r]] for r in range(2)]

    def grad_columns(rels):
        cut = lambda rel: lax.dynamic_slice_in_dim(g0, (chip ^ rel) * 2 * width, 2 * width, 1)
        return jnp.concatenate([cut(rel) for rel in rels], axis=1)

    q_both = halve(meta, after(q0, kvs0[nc - 2], kvs1[nc - 2]), q1)
    kvs0[-1], kvs1[-1] = after(kvs0[-1], q_both), after(kvs1[-1], q_both)
    kvs = kvs0 + kvs1
    a_both, *at, st = forward(block_list, block_count, meta, q_both, kvs)
    near_grads = []
    for r in range(2):
        got = to_chip(after(grad_columns(with_bit[r]), *w_gate, a_both), routes[r][0])
        near_grads.append((got, to_core(got)))
    far_at = [to_chip(after(at[r], near_grads[r][0]), routes[r][0]) for r in range(2)]
    def total(parts):
        return functools.reduce(jnp.add, [x.astype(F32) for x in parts])

    class Chain:
        def __init__(self, shard, sign):
            self.shard, self.sign, self.step = shard, sign, 0

        def send(self):
            self.step += 1
            t = jnp.clip(c - self.sign * (self.step - nc), 0, nc - 1)
            own = self.shard(t)
            self.sent = own if self.step == 1 else total([own, self.got]).astype(BF16)
            reach = [p for p in range(nc) if (nc - 1 - p if self.sign < 0 else p) < self.step]
            pairs = [(p, p + self.sign) for p in reach if 0 <= p + self.sign < nc]
            self.got = lax.ppermute(self.sent, "ctx", pairs)

        def gate(self, *earlier):
            self.got = after(self.got, *earlier)

        def result(self):
            while self.step < nc - 1:
                self.send()
            return self.got

    kv_shard = lambda dkv: lambda t: lax.dynamic_slice_in_dim(dkv, t * rows, rows, 1)
    listed = (block_list, block_count, meta)
    dq1, dkv1, do0 = backward(*listed, 1, q_both, a_both, st, kvs1, (g0, g1, *arrays), plan)

    def hop_down(step, got):
        parts = []
        for lane, dkv in ((0, dkv1), (1, dkv0)):
            hop = step - lane
            if 1 <= hop < nc:
                own = kv_shard(dkv)(jnp.maximum(c + hop - nc, 0))
                parts.append(own if hop == 1 else total([own, got[lane]]).astype(BF16))
            else:
                parts.append(None)
        sending = jnp.stack([x for x in parts if x is not None])
        moved = lax.ppermute(sending, "ctx", [(p, p - 1) for p in range(max(nc - step, 1), nc)])
        return sending, moved

    def unpack(step, moved):
        return (moved[0] if step < nc else None, moved[-1] if step > 1 else None)

    dkv0 = None
    sending, moved = hop_down(1, None)
    dq0, dkv0 = backward(*listed, 0, after(q_both, sending), a_both, st, kvs0, (do0,))
    sending, moved = hop_down(2, unpack(1, after(moved, dkv0)))

    inputs = []
    for r in range(2):
        inputs += [at[r], after(far_at[r], dkv0), *near_grads[r]]
    order = [
        [[jnp.stack([((chip ^ rel) * 2 + (core ^ side)) * width, (n * 2 + (core ^ side)) * width]) for side in range(2)]
         for n, rel in enumerate(without[r])]
        for r in range(2)
    ]
    cols = jnp.stack([jnp.stack([jnp.stack(pair) for pair in route]) for route in order]).astype(jnp.int32)
    parts = proj_parts(after(cols, sending), g0, g1, inputs, width)
    count = len(without[0])
    own_mix, other_mix = mix(meta, after(a_both, parts[0]), resid[0], plan, arrays)
    sending, moved = hop_down(3, unpack(2, after(moved, other_mix)))
    for step in range(4, nc + 1):
        if step == nc:
            sum1 = total([kv_shard(dkv1)(c), moved[0]]).astype(BF16)
        sending_more, moved = hop_down(step, unpack(step - 1, moved))
    sum0 = total([kv_shard(dkv0)(c), moved[-1]]).astype(BF16)
    query_grad = place(dq0, to_core(after(dq1, other_mix)), 1)[None]

    def reduce_chips(r):
        have = {(rel, side): parts[(r * count + n) * 2 + side] for n, rel in enumerate(without[r]) for side in range(2)}
        for bit in routes[r][1:-1]:
            far = sorted({rel for rel, _ in have if rel & bit})
            for side in range(2):
                got = to_chip(jnp.stack([have.pop((rel, side)).astype(BF16) for rel in far]), bit)
                for n, rel in enumerate(far):
                    have[rel ^ bit, side] = total([have[rel ^ bit, side], got[n]])
        bit = routes[r][-1]
        same = to_chip(have[bit, 0].astype(BF16), bit)
        cross = lax.ppermute(have[bit, 1].astype(BF16), "fsdp", [(p, p ^ (2 * bit) ^ 1) for p in range(nf)])
        return have[0, 0], have[0, 1], after(same, other_mix), after(cross, other_mix)

    reduced = [reduce_chips(r) for r in range(2)]
    swapped = to_core(after(jnp.concatenate([part[1].astype(BF16) for part in reduced], axis=0), other_mix))
    mine = [total([near, same]) for near, _, same, _ in reduced]
    theirs = [total([swapped[r * mid:(r + 1) * mid], reduced[r][3]]) for r in range(2)]
    proj_rows = jnp.concatenate(mine + theirs, axis=0).astype(BF16)
    proj_rows = after(proj_rows, sending)
    share = QUERY_HEADS * HEAD_DIM // nc

    def proj_shard(t):
        start = t * share
        return lax.dynamic_slice_in_dim(proj_rows, start + (core * HALF) * jnp.where(start < HALF, 1, -1), share, 0)

    proj_down, proj_up = Chain(proj_shard, -1), Chain(proj_shard, 1)
    for _ in range(nc - 1):
        proj_down.send()
        proj_up.send()
        proj_down.got, proj_up.got = lax.optimization_barrier((proj_down.got, proj_up.got))
    proj_grad = total([proj_shard(c), proj_down.got, proj_up.got])
    mixed = total([own_mix, to_core(other_mix)]).astype(BF16)
    grads = place(sum0, to_core(sum1), 2)
    return mixed[None], query_grad, grads[:1], grads[1:], proj_grad


def solution(mesh):
    rows = P("fsdp", "ctx", None)
    body = functools.partial(local, mesh.shape["ctx"], mesh.shape["fsdp"])
    return jax.shard_map(
        body,
        mesh=mesh,
        in_specs=(rows, rows, rows, rows, rows, P(None, "fsdp"), P("ctx", None), P("ctx")),
        out_specs=(rows, rows, rows, rows, P("ctx", "fsdp")),
        check_vma=False,
    )
```

```python
import functools
import math

import jax
import jax.numpy as jnp
from jax import lax
from jax.experimental import pallas as pl
from jax.experimental.pallas import tpu as pltpu
from jax.sharding import PartitionSpec as P

QUERY_HEADS = 16
KEY_VALUE_HEADS = 4
HEAD_DIM = 128
BLOCK_SIZE = 128
KEY_SLOTS = 8

GROUP = QUERY_HEADS // KEY_VALUE_HEADS
CORE_KV = KEY_VALUE_HEADS // 2
HALF = QUERY_HEADS * HEAD_DIM // 2
KV_HALF = CORE_KV * HEAD_DIM
STACK = GROUP * BLOCK_SIZE
WIDE = GROUP * HEAD_DIM
SCALE = 1.0 / math.sqrt(HEAD_DIM)
EXP2_SCALE = SCALE * math.log2(math.e)
NEG = -1e30
F32 = jnp.float32
BF16 = jnp.bfloat16
VMEM_LIMIT = 56 * 1024 * 1024
NT = (((1,), (1,)), ((), ()))
TN = (((0,), (0,)), ((), ()))


def dot(a, b):
    return jnp.dot(a, b, preferred_element_type=F32)


def stack_heads(x):
    return jnp.concatenate([x[:, h * HEAD_DIM:(h + 1) * HEAD_DIM] for h in range(GROUP)], axis=0)


def cost(weight):
    return pl.CostEstimate(flops=int(weight * 1e9), bytes_accessed=1_000_000, transcendentals=0)


def params(steps):
    return pltpu.CompilerParams(dimension_semantics=("arbitrary",) * steps, vmem_limit_bytes=VMEM_LIMIT)


def fill_kv(kv_refs, kv_sc, rows, nc):
    for n, ref in enumerate(kv_refs):
        d = n % nc
        for u in range(2 * CORE_KV):
            kv_sc[n // nc, u, d * rows:(d + 1) * rows, :] = ref[:, u * HEAD_DIM:(u + 1) * HEAD_DIM]


def slot_rows(bl_ref, c, i, j, nb):
    b = bl_ref[i, j]
    chip = b // nb
    return pl.multiple_of(((c - chip) * nb + (b - chip * nb)) * BLOCK_SIZE, BLOCK_SIZE)


def masked_scores(k_cat, qs, slots, count):
    s_t = lax.dot_general(k_cat, qs, NT, preferred_element_type=F32)
    key = lax.broadcasted_iota(jnp.int32, (BLOCK_SIZE, STACK), 0)
    query = lax.broadcasted_iota(jnp.int32, (BLOCK_SIZE, STACK), 1) & (BLOCK_SIZE - 1)
    parts = [jnp.where(key <= query, s_t[:BLOCK_SIZE], NEG)]
    for j in range(1, slots):
        parts.append(jnp.where(j < count, s_t[j * BLOCK_SIZE:(j + 1) * BLOCK_SIZE], NEG))
    return jnp.concatenate(parts, axis=0)


def by_count(count, run):
    quarter = KEY_SLOTS // 4
    for n in range(1, 5):

        @pl.when((count > (n - 1) * quarter) & (count <= n * quarter))
        def _(n=n):
            run(n * quarter)


def wide_part(ref, g):
    return stack_heads(ref[0, :, g * WIDE:(g + 1) * WIDE])


def slot_cat(kv_sc, s, u, starts):
    return jnp.concatenate([kv_sc[s, u, pl.ds(at, BLOCK_SIZE), :] for at in starts], axis=0)


def forward_kernel(nc, nb, bl_ref, bc_ref, meta_ref, q_ref, *rest):
    kv_refs, (a_ref, *at_refs, st_ref, kv_sc) = rest[:2 * nc], rest[2 * nc:]
    step = pl.program_id(0)
    s, i = step // nb, step % nb

    @pl.when(step == 0)
    def _():
        fill_kv(kv_refs, kv_sc, nb * BLOCK_SIZE, nc)

    c = meta_ref[0]
    count = bc_ref[i]

    def run(slots):
        starts = [slot_rows(bl_ref, c, i, j, nb) for j in range(slots)]
        for g in range(CORE_KV):
            qs = wide_part(q_ref, g)
            k_cat = slot_cat(kv_sc, s, g, starts)
            v_cat = slot_cat(kv_sc, s, CORE_KV + g, starts)
            s_t = masked_scores(k_cat, qs, slots, count)
            top = jnp.max(s_t, axis=0, keepdims=True)
            p = jnp.exp2((s_t - top) * EXP2_SCALE)
            total = jnp.sum(p, axis=0, keepdims=True)
            a_t = lax.dot_general(v_cat, p.astype(BF16), TN, preferred_element_type=F32) / total
            st_ref[0, g] = top * EXP2_SCALE + jnp.log2(total)
            for h in range(GROUP):
                part = a_t[:, h * BLOCK_SIZE:(h + 1) * BLOCK_SIZE]
                at_refs[g][0, h * HEAD_DIM:(h + 1) * HEAD_DIM, :] = part.astype(BF16)
                lane = g * WIDE + h * HEAD_DIM
                a_ref[0, :, lane:lane + HEAD_DIM] = part.astype(BF16).T

    by_count(count, run)


def kv_specs(nc, rows):
    return [pl.BlockSpec((rows, 2 * KV_HALF), lambda n, *_: (0, 0)) for _ in range(2 * nc)]


def forward(bl, bc, meta, q, kvs, weight=20):
    nc, rows = len(kvs) // 2, q.shape[1]
    nb = rows // BLOCK_SIZE
    wide = pl.BlockSpec((1, BLOCK_SIZE, HALF), lambda n, *_: (n // nb, n % nb, 0))
    turned = pl.BlockSpec((1, WIDE, BLOCK_SIZE), lambda n, *_: (n // nb, 0, n % nb))
    return pl.pallas_call(
        functools.partial(forward_kernel, nc, nb),
        grid_spec=pltpu.PrefetchScalarGridSpec(
            num_scalar_prefetch=3,
            grid=(2 * nb,),
            in_specs=[wide, *kv_specs(nc, rows)],
            out_specs=[wide, *[turned] * CORE_KV, pl.BlockSpec((1, CORE_KV, 1, STACK), lambda n, *_: (n, 0, 0, 0))],
            scratch_shapes=[pltpu.VMEM((2, 2 * CORE_KV, nc * rows, HEAD_DIM), BF16)],
        ),
        out_shape=[
            jax.ShapeDtypeStruct((2, rows, HALF), BF16),
            *[jax.ShapeDtypeStruct((2, WIDE, rows), BF16)] * CORE_KV,
            jax.ShapeDtypeStruct((2 * nb, CORE_KV, 1, STACK), F32),
        ],
        compiler_params=params(1),
        cost_estimate=cost(weight),
        name="attention_forward",
    )(bl, bc, meta, q, *kvs)


def backward_kernel(nc, nb, plan, width, bl_ref, bc_ref, meta_ref, q_ref, a_ref, st_ref, *rest):
    kv_refs, rest = rest[:nc], rest[nc:]
    if plan:
        (g0_ref, g1_ref, *w_refs), (dq_ref, dkv_ref, spare_ref, kv_sc, acc, do_ref) = rest[:-6], rest[-6:]
    else:
        do_ref, dq_ref, dkv_ref, kv_sc, acc = rest
    i = pl.program_id(0)
    rows = nb * BLOCK_SIZE

    @pl.when(i == 0)
    def _():
        if plan:
            for span, part in output_grad_product(plan, width, meta_ref, (g0_ref, g1_ref), w_refs):
                spare_ref[:, span] = part[:rows].astype(BF16)
                do_ref[:, span] = part[rows:].astype(BF16)
        fill_kv(kv_refs, kv_sc, rows, nc)
        acc[...] = jnp.zeros_like(acc)

    c = meta_ref[0]
    count = bc_ref[i]

    def run(slots):
        starts = [slot_rows(bl_ref, c, i, j, nb) for j in range(slots)]
        here = pl.ds(pl.multiple_of(i * BLOCK_SIZE, BLOCK_SIZE), BLOCK_SIZE)
        for g in range(CORE_KV):
            qs = wide_part(q_ref, g)
            dos = stack_heads(do_ref[here, g * WIDE:(g + 1) * WIDE])
            outs = wide_part(a_ref, g)
            row_dot = jnp.sum((dos.astype(F32) * outs.astype(F32)).T, axis=0, keepdims=True)
            k_cat = slot_cat(kv_sc, 0, g, starts)
            v_cat = slot_cat(kv_sc, 0, CORE_KV + g, starts)
            s_t = masked_scores(k_cat, qs, slots, count)
            p = jnp.exp2(s_t * EXP2_SCALE - st_ref[0, g])
            dp = lax.dot_general(v_cat, dos, NT, preferred_element_type=F32)
            ds = (p * (dp - row_dot)).astype(BF16)
            dv = dot(p.astype(BF16), dos)
            dk = dot(ds, qs) * SCALE
            dq_t = lax.dot_general(k_cat, ds, TN, preferred_element_type=F32) * SCALE
            for h in range(GROUP):
                part = dq_t[:, h * BLOCK_SIZE:(h + 1) * BLOCK_SIZE]
                lane = g * WIDE + h * HEAD_DIM
                dq_ref[:, lane:lane + HEAD_DIM] = part.astype(BF16).T
            lanes = slice(g * HEAD_DIM, (g + 1) * HEAD_DIM)
            for j in range(slots):
                at = pl.ds(pl.multiple_of(bl_ref[i, j] * BLOCK_SIZE, BLOCK_SIZE), BLOCK_SIZE)
                acc[0, at, lanes] += dk[j * BLOCK_SIZE:(j + 1) * BLOCK_SIZE]
                acc[1, at, lanes] += dv[j * BLOCK_SIZE:(j + 1) * BLOCK_SIZE]

    by_count(count, run)

    @pl.when(i == nb - 1)
    def _():
        dkv_ref[...] = acc[...].astype(BF16)


def backward(bl, bc, meta, s, q, a, st, kvs, extra, plan=(), weight=20):
    nc, rows = len(kvs), q.shape[1]
    nb, width = rows // BLOCK_SIZE, extra[-1].shape[-1]
    wide = pl.BlockSpec((1, BLOCK_SIZE, HALF), lambda n, *_: (s, n, 0))
    whole = pl.BlockSpec(memory_space=pltpu.VMEM)
    grad = jax.ShapeDtypeStruct((rows, HALF), BF16)
    return pl.pallas_call(
        functools.partial(backward_kernel, nc, nb, plan, width),
        grid_spec=pltpu.PrefetchScalarGridSpec(
            num_scalar_prefetch=3,
            grid=(nb,),
            in_specs=[
                wide,
                wide,
                pl.BlockSpec((1, CORE_KV, 1, STACK), lambda n, *_: (s * nb + n, 0, 0, 0)),
                *[whole] * (nc + len(extra)),
            ],
            out_specs=[
                pl.BlockSpec((BLOCK_SIZE, HALF), lambda n, *_: (n, 0)),
                pl.BlockSpec((2, nc * rows, KV_HALF), lambda n, *_: (0, 0, 0)),
                *[pl.BlockSpec((rows, HALF), lambda n, *_: (0, 0))] * bool(plan),
            ],
            scratch_shapes=[
                pltpu.VMEM((1, 2 * CORE_KV, nc * rows, HEAD_DIM), BF16),
                pltpu.VMEM((2, nc * rows, KV_HALF), F32),
                *[pltpu.VMEM((rows, HALF), BF16)] * bool(plan),
            ],
        ),
        out_shape=[grad, jax.ShapeDtypeStruct((2, nc * rows, KV_HALF), BF16), *[grad] * bool(plan)],
        compiler_params=params(1),
        cost_estimate=cost(weight),
        name="attention_backward",
    )(bl, bc, meta, q, a, st, *kvs, *extra)


def column(meta_ref, chip, core, width):
    at = ((meta_ref[2] ^ chip) * 2 + (meta_ref[1] ^ core)) * width
    return pl.ds(pl.multiple_of(at, width), width)


def read_piece(w_refs, piece):
    ref, lead, start = piece
    rows = pl.ds(start, HALF // 2)
    return w_refs[ref][rows, :] if lead is None else w_refs[ref][lead, rows, :]


def output_grad_product(plan, width, meta_ref, g_refs, w_refs):
    grads = jnp.concatenate(
        [
            jnp.concatenate([ref[:, column(meta_ref, chip, core, width)] for ref in g_refs], axis=0)
            for chip, core, _ in plan
        ],
        axis=1,
    )
    for r in range(2):
        w = jnp.concatenate([read_piece(w_refs, pieces[r]) for _, _, pieces in plan], axis=1)
        yield slice(r * (HALF // 2), (r + 1) * (HALF // 2)), lax.dot_general(
            grads, w, NT, preferred_element_type=F32
        )


def mix_kernel(plan, width, meta_ref, a_ref, resid_ref, *rest):
    w_refs, (own_ref, other_ref) = rest[:-2], rest[-2:]
    rows = resid_ref.shape[0]
    a = jnp.concatenate([a_ref[0], a_ref[1]], axis=0)
    for chip, core, pieces in plan:
        at = column(meta_ref, chip, core, width)
        part = dot(a, jnp.concatenate([read_piece(w_refs, piece) for piece in pieces], axis=0))
        own_ref[:, at] = part[:rows] + resid_ref[:, at].astype(F32)
        other_ref[:, at] = part[rows:].astype(BF16)


def mix(meta, a, resid, plan, arrays, weight=20):
    width = arrays[0].shape[-1]
    whole = pl.BlockSpec(memory_space=pltpu.VMEM)
    return pl.pallas_call(
        functools.partial(mix_kernel, plan, width),
        in_specs=[pl.BlockSpec(memory_space=pltpu.SMEM)] + [whole] * (2 + len(arrays)),
        out_specs=[whole, whole],
        out_shape=[jax.ShapeDtypeStruct(resid.shape, F32), jax.ShapeDtypeStruct(resid.shape, BF16)],
        compiler_params=params(0),
        cost_estimate=cost(weight),
        name="mix",
    )(meta, a, resid, *arrays)


def proj_kernel(count, width, cols_ref, g0_ref, g1_ref, *refs):
    inputs, outputs = refs[:8], refs[8:]
    for r in range(2):
        at_ref, far_ref, near0_ref, near1_ref = inputs[4 * r:4 * r + 4]
        lhs = jnp.concatenate([at_ref[0], at_ref[1], far_ref[0], far_ref[1]], axis=1)
        for n in range(count):
            for side in range(2):
                own = pl.ds(pl.multiple_of(cols_ref[r, n, side, 0], width), width)
                near = pl.ds(pl.multiple_of(cols_ref[r, n, side, 1], width), width)
                rhs = [g0_ref[:, own], g1_ref[:, own], near0_ref[:, near], near1_ref[:, near]]
                out = dot(lhs, jnp.concatenate(rhs, axis=0))
                outputs[(r * count + n) * 2 + side][...] = out.astype(BF16)


def proj_parts(cols, g0, g1, inputs, width, weight=20):
    count = cols.shape[1]
    whole = pl.BlockSpec(memory_space=pltpu.VMEM)
    return pl.pallas_call(
        functools.partial(proj_kernel, count, width),
        in_specs=[pl.BlockSpec(memory_space=pltpu.SMEM)] + [whole] * 10,
        out_specs=[whole] * (4 * count),
        out_shape=[jax.ShapeDtypeStruct((WIDE, width), BF16)] * (4 * count),
        compiler_params=params(0),
        cost_estimate=cost(weight),
        name="proj_parts",
    )(cols, g0, g1, *inputs)


def halve_kernel(meta_ref, q0_ref, q1_ref, out_ref):
    out_ref[0] = q0_ref[...]
    out_ref[1] = q1_ref[...]


def halve(meta, q0, q1, weight=20):
    rows = q0.shape[0]
    half = pl.BlockSpec((rows, HALF), lambda n, m: (0, m[1]))
    return pl.pallas_call(
        halve_kernel,
        grid_spec=pltpu.PrefetchScalarGridSpec(
            num_scalar_prefetch=1,
            grid=(1,),
            in_specs=[half, half],
            out_specs=pl.BlockSpec((2, rows, HALF), lambda n, m: (0, 0, 0)),
        ),
        out_shape=jax.ShapeDtypeStruct((2, rows, HALF), BF16),
        compiler_params=params(1),
        cost_estimate=cost(weight),
        name="halve",
    )(meta, q0, q1)


def after(x, *earlier):
    return lax.optimization_barrier((x, *earlier))[0]


def local(nc, nf, queries, keys, values, resid, grad_out, w_out, block_list, block_count):
    chips = nf // 2
    bits = [1 << b for b in range(chips.bit_length() - 1)]
    routes = (bits, bits[::-1])
    mid = HALF // 2
    c = lax.axis_index("ctx")
    f = lax.axis_index("fsdp")
    core, chip = f % 2, f // 2
    meta = jnp.stack([c, core, chip]).astype(jnp.int32)
    rows = queries.shape[1]
    width = w_out.shape[1]

    def to_core(x):
        return lax.ppermute(x, "fsdp", [(p, p ^ 1) for p in range(nf)])

    def to_chip(x, bit):
        return lax.ppermute(x, "fsdp", [(p, p ^ (2 * bit)) for p in range(nf)])

    def place(mine, theirs, axis):
        return jnp.where(
            core == 0,
            jnp.concatenate([mine, theirs], axis=axis),
            jnp.concatenate([theirs, mine], axis=axis),
        )

    def kv_part(which):
        cut = lambda x: lax.dynamic_slice_in_dim(x[0], which * KV_HALF, KV_HALF, 1)
        return jnp.concatenate([cut(keys), cut(values)], axis=1)

    def hop_up(x, step):
        return lax.ppermute(x, "ctx", [(p, p + 1) for p in range(step - 1, nc - 1)])

    q0, g0 = queries[0], grad_out[0]
    w_mine = lax.dynamic_slice_in_dim(w_out, core * HALF, HALF, 0)
    kvs0 = [kv_part(core)]
    kvs1 = [to_core(kv_part(1 - core))]
    w_theirs = to_core(lax.dynamic_slice_in_dim(w_out, (1 - core) * HALF, HALF, 0))

    arrays = [w_mine, w_theirs]
    held = {(0, side, r): (side, None, r * mid) for side in range(2) for r in range(2)}
    last = {}
    for side in range(2):
        for bit in bits:
            got = to_chip(after(arrays[side], *last.get(bit, ())), bit)
            for r in range(2):
                held[bit, side, r] = (len(arrays), None, r * mid)
            arrays.append(got)
            last[bit] = (got,)
    for step in range(1, nc):
        kvs0.append(hop_up(kvs0[-1], step))
        kvs1.append(hop_up(kvs1[-1], step))
    for step in range(1, len(bits)):
        for r in range(2):
            bit = routes[r][step]
            known = [0]
            for earlier in routes[r][:step]:
                known += [rel ^ earlier for rel in known]
            sources = [(rel, side) for rel in known[1:] for side in range(2)]
            parts = []
            for source in sources:
                ref, lead, first = held[(*source, r)]
                x = arrays[ref] if lead is None else arrays[ref][lead]
                parts.append(x[first:first + mid])
            got = to_chip(after(jnp.stack(parts), *last[bit], kvs0[nc - 2], kvs1[nc - 2]), bit)
            for n, (rel, side) in enumerate(sources):
                held[rel ^ bit, side, r] = (len(arrays), n, 0)
            arrays.append(got)
            last[bit] = (got,)
    w_gate = [x for bit in bits for x in last[bit]]
    g1 = to_core(after(g0, w_theirs, kvs1[0]))
    q1 = to_core(after(q0, g1))
    plan = [
        (rel, core_bit, [held[rel, core_bit, r] for r in range(2)]) for rel in range(chips) for core_bit in range(2)
    ]
    with_bit = [[rel for rel in range(chips) if rel & route[0]] for route in routes]
    without = [[rel ^ routes[r][0] for rel in with_bit[r]] for r in range(2)]

    def grad_columns(rels):
        cut = lambda rel: lax.dynamic_slice_in_dim(g0, (chip ^ rel) * 2 * width, 2 * width, 1)
        return jnp.concatenate([cut(rel) for rel in rels], axis=1)

    q_both = halve(meta, after(q0, kvs0[nc - 2], kvs1[nc - 2]), q1)
    kvs0[-1], kvs1[-1] = after(kvs0[-1], q_both), after(kvs1[-1], q_both)
    kvs = kvs0 + kvs1
    a_both, *at, st = forward(block_list, block_count, meta, q_both, kvs)
    near_grads = []
    for r in range(2):
        got = to_chip(after(grad_columns(with_bit[r]), *w_gate, a_both), routes[r][0])
        near_grads.append((got, to_core(got)))
    far_at = [to_chip(after(at[r], near_grads[r][0]), routes[r][0]) for r in range(2)]
    def total(parts):
        return functools.reduce(jnp.add, [x.astype(F32) for x in parts])

    class Chain:
        def __init__(self, shard, sign):
            self.shard, self.sign, self.step = shard, sign, 0

        def send(self):
            self.step += 1
            t = jnp.clip(c - self.sign * (self.step - nc), 0, nc - 1)
            own = self.shard(t)
            self.sent = own if self.step == 1 else total([own, self.got]).astype(BF16)
            reach = [p for p in range(nc) if (nc - 1 - p if self.sign < 0 else p) < self.step]
            pairs = [(p, p + self.sign) for p in reach if 0 <= p + self.sign < nc]
            self.got = lax.ppermute(self.sent, "ctx", pairs)

        def gate(self, *earlier):
            self.got = after(self.got, *earlier)

        def result(self):
            while self.step < nc - 1:
                self.send()
            return self.got

    kv_shard = lambda dkv: lambda t: lax.dynamic_slice_in_dim(dkv, t * rows, rows, 1)
    listed = (block_list, block_count, meta)
    dq1, dkv1, do0 = backward(*listed, 1, q_both, a_both, st, kvs1, (g0, g1, *arrays), plan)

    def hop_down(step, got):
        parts = []
        for lane, dkv in ((0, dkv1), (1, dkv0)):
            hop = step - lane
            if 1 <= hop < nc:
                own = kv_shard(dkv)(jnp.maximum(c + hop - nc, 0))
                parts.append(own if hop == 1 else total([own, got[lane]]).astype(BF16))
            else:
                parts.append(None)
        sending = jnp.stack([x for x in parts if x is not None])
        moved = lax.ppermute(sending, "ctx", [(p, p - 1) for p in range(max(nc - step, 1), nc)])
        return sending, moved

    def unpack(step, moved):
        return (moved[0] if step < nc else None, moved[-1] if step > 1 else None)

    dkv0 = None
    sending, moved = hop_down(1, None)
    dq0, dkv0 = backward(*listed, 0, after(q_both, sending), a_both, st, kvs0, (do0,))
    sending, moved = hop_down(2, unpack(1, after(moved, dkv0)))

    inputs = []
    for r in range(2):
        inputs += [at[r], after(far_at[r], dkv0), *near_grads[r]]
    order = [
        [[jnp.stack([((chip ^ rel) * 2 + (core ^ side)) * width, (n * 2 + (core ^ side)) * width]) for side in range(2)]
         for n, rel in enumerate(without[r])]
        for r in range(2)
    ]
    cols = jnp.stack([jnp.stack([jnp.stack(pair) for pair in route]) for route in order]).astype(jnp.int32)
    parts = proj_parts(after(cols, sending), g0, g1, inputs, width)
    count = len(without[0])
    own_mix, other_mix = mix(meta, after(a_both, parts[0]), resid[0], plan, arrays)
    sending, moved = hop_down(3, unpack(2, after(moved, other_mix)))
    for step in range(4, nc + 1):
        if step == nc:
            sum1 = total([kv_shard(dkv1)(c), moved[0]]).astype(BF16)
        sending_more, moved = hop_down(step, unpack(step - 1, moved))
    sum0 = total([kv_shard(dkv0)(c), moved[-1]]).astype(BF16)
    query_grad = place(dq0, to_core(after(dq1, other_mix)), 1)[None]

    def reduce_chips(r):
        have = {(rel, side): parts[(r * count + n) * 2 + side] for n, rel in enumerate(without[r]) for side in range(2)}
        for bit in routes[r][1:-1]:
            far = sorted({rel for rel, _ in have if rel & bit})
            for side in range(2):
                got = to_chip(jnp.stack([have.pop((rel, side)).astype(BF16) for rel in far]), bit)
                for n, rel in enumerate(far):
                    have[rel ^ bit, side] = total([have[rel ^ bit, side], got[n]])
        bit = routes[r][-1]
        same = to_chip(have[bit, 0].astype(BF16), bit)
        cross = lax.ppermute(have[bit, 1].astype(BF16), "fsdp", [(p, p ^ (2 * bit) ^ 1) for p in range(nf)])
        return have[0, 0], have[0, 1], after(same, other_mix), after(cross, other_mix)

    reduced = [reduce_chips(r) for r in range(2)]
    swapped = to_core(after(jnp.concatenate([part[1].astype(BF16) for part in reduced], axis=0), other_mix))
    mine = [total([near, same]) for near, _, same, _ in reduced]
    theirs = [total([swapped[r * mid:(r + 1) * mid], reduced[r][3]]) for r in range(2)]
    proj_rows = jnp.concatenate(mine + theirs, axis=0).astype(BF16)
    proj_rows = after(proj_rows, sending)
    share = QUERY_HEADS * HEAD_DIM // nc

    def proj_shard(t):
        start = t * share
        return lax.dynamic_slice_in_dim(proj_rows, start + (core * HALF) * jnp.where(start < HALF, 1, -1), share, 0)

    proj_down, proj_up = Chain(proj_shard, -1), Chain(proj_shard, 1)
    for _ in range(nc - 1):
        proj_down.send()
        proj_up.send()
        proj_down.got, proj_up.got = lax.optimization_barrier((proj_down.got, proj_up.got))
    proj_grad = total([proj_shard(c), proj_down.got, proj_up.got])
    mixed = total([own_mix, to_core(other_mix)]).astype(BF16)
    grads = place(sum0, to_core(sum1), 2)
    return mixed[None], query_grad, grads[:1], grads[1:], proj_grad


def solution(mesh):
    rows = P("fsdp", "ctx", None)
    body = functools.partial(local, mesh.shape["ctx"], mesh.shape["fsdp"])
    return jax.shard_map(
        body,
        mesh=mesh,
        in_specs=(rows, rows, rows, rows, rows, P(None, "fsdp"), P("ctx", None), P("ctx")),
        out_specs=(rows, rows, rows, rows, P("ctx", "fsdp")),
        check_vma=False,
    )
```

```python
import functools
import math

import jax
import jax.numpy as jnp
from jax import lax
from jax.experimental import pallas as pl
from jax.experimental.pallas import tpu as pltpu
from jax.sharding import PartitionSpec as P

QUERY_HEADS = 16
KEY_VALUE_HEADS = 4
HEAD_DIM = 128
BLOCK_SIZE = 128
KEY_SLOTS = 8

GROUP = QUERY_HEADS // KEY_VALUE_HEADS
CORE_KV = KEY_VALUE_HEADS // 2
HALF = QUERY_HEADS * HEAD_DIM // 2
KV_HALF = CORE_KV * HEAD_DIM
STACK = GROUP * BLOCK_SIZE
WIDE = GROUP * HEAD_DIM
SCALE = 1.0 / math.sqrt(HEAD_DIM)
EXP2_SCALE = SCALE * math.log2(math.e)
NEG = -1e30
F32 = jnp.float32
BF16 = jnp.bfloat16
VMEM_LIMIT = 56 * 1024 * 1024
NT = (((1,), (1,)), ((), ()))
TN = (((0,), (0,)), ((), ()))


def dot(a, b):
    return jnp.dot(a, b, preferred_element_type=F32)


def stack_heads(x):
    return jnp.concatenate([x[:, h * HEAD_DIM:(h + 1) * HEAD_DIM] for h in range(GROUP)], axis=0)


def cost(weight):
    return pl.CostEstimate(flops=int(weight * 1e9), bytes_accessed=1_000_000, transcendentals=0)


def params(steps):
    return pltpu.CompilerParams(dimension_semantics=("arbitrary",) * steps, vmem_limit_bytes=VMEM_LIMIT)


def fill_kv(kv_refs, kv_sc, rows, nc):
    for n, ref in enumerate(kv_refs):
        d = n % nc
        for u in range(2 * CORE_KV):
            kv_sc[n // nc, u, d * rows:(d + 1) * rows, :] = ref[:, u * HEAD_DIM:(u + 1) * HEAD_DIM]


def slot_rows(bl_ref, c, i, j, nb):
    b = bl_ref[i, j]
    chip = b // nb
    return pl.multiple_of(((c - chip) * nb + (b - chip * nb)) * BLOCK_SIZE, BLOCK_SIZE)


def masked_scores(k_cat, qs, slots, count):
    s_t = lax.dot_general(k_cat, qs, NT, preferred_element_type=F32)
    key = lax.broadcasted_iota(jnp.int32, (BLOCK_SIZE, STACK), 0)
    query = lax.broadcasted_iota(jnp.int32, (BLOCK_SIZE, STACK), 1) & (BLOCK_SIZE - 1)
    parts = [jnp.where(key <= query, s_t[:BLOCK_SIZE], NEG)]
    parts.append(s_t[BLOCK_SIZE:(slots - 1) * BLOCK_SIZE])
    parts.append(jnp.where(slots <= count, s_t[(slots - 1) * BLOCK_SIZE:], NEG))
    return jnp.concatenate([part for part in parts if part.shape[0]], axis=0)


def by_count(count, run):
    quarter = KEY_SLOTS // 4
    for n in range(1, 5):

        @pl.when((count > (n - 1) * quarter) & (count <= n * quarter))
        def _(n=n):
            run(n * quarter)


def wide_part(ref, g):
    return stack_heads(ref[0, :, g * WIDE:(g + 1) * WIDE])


def slot_cat(kv_sc, s, u, starts):
    return jnp.concatenate([kv_sc[s, u, pl.ds(at, BLOCK_SIZE), :] for at in starts], axis=0)


def forward_kernel(nc, nb, bl_ref, bc_ref, meta_ref, q_ref, *rest):
    kv_refs, (a_ref, *at_refs, st_ref, kv_sc) = rest[:2 * nc], rest[2 * nc:]
    step = pl.program_id(0)
    s, i = step // nb, step % nb

    @pl.when(step == 0)
    def _():
        fill_kv(kv_refs, kv_sc, nb * BLOCK_SIZE, nc)

    c = meta_ref[0]
    count = bc_ref[i]

    def run(slots):
        starts = [slot_rows(bl_ref, c, i, j, nb) for j in range(slots)]
        for g in range(CORE_KV):
            qs = wide_part(q_ref, g)
            k_cat = slot_cat(kv_sc, s, g, starts)
            v_cat = slot_cat(kv_sc, s, CORE_KV + g, starts)
            s_t = masked_scores(k_cat, qs, slots, count)
            top = jnp.max(s_t, axis=0, keepdims=True)
            p = jnp.exp2((s_t - top) * EXP2_SCALE)
            total = jnp.sum(p, axis=0, keepdims=True)
            a_t = lax.dot_general(v_cat, p.astype(BF16), TN, preferred_element_type=F32) / total
            st_ref[0, g] = top * EXP2_SCALE + jnp.log2(total)
            for h in range(GROUP):
                part = a_t[:, h * BLOCK_SIZE:(h + 1) * BLOCK_SIZE]
                at_refs[g][0, h * HEAD_DIM:(h + 1) * HEAD_DIM, :] = part.astype(BF16)
                lane = g * WIDE + h * HEAD_DIM
                a_ref[0, :, lane:lane + HEAD_DIM] = part.astype(BF16).T

    by_count(count, run)


def kv_specs(nc, rows):
    return [pl.BlockSpec((rows, 2 * KV_HALF), lambda n, *_: (0, 0)) for _ in range(2 * nc)]


def forward(bl, bc, meta, q, kvs, weight=20):
    nc, rows = len(kvs) // 2, q.shape[1]
    nb = rows // BLOCK_SIZE
    wide = pl.BlockSpec((1, BLOCK_SIZE, HALF), lambda n, *_: (n // nb, n % nb, 0))
    turned = pl.BlockSpec((1, WIDE, BLOCK_SIZE), lambda n, *_: (n // nb, 0, n % nb))
    return pl.pallas_call(
        functools.partial(forward_kernel, nc, nb),
        grid_spec=pltpu.PrefetchScalarGridSpec(
            num_scalar_prefetch=3,
            grid=(2 * nb,),
            in_specs=[wide, *kv_specs(nc, rows)],
            out_specs=[wide, *[turned] * CORE_KV, pl.BlockSpec((1, CORE_KV, 1, STACK), lambda n, *_: (n, 0, 0, 0))],
            scratch_shapes=[pltpu.VMEM((2, 2 * CORE_KV, nc * rows, HEAD_DIM), BF16)],
        ),
        out_shape=[
            jax.ShapeDtypeStruct((2, rows, HALF), BF16),
            *[jax.ShapeDtypeStruct((2, WIDE, rows), BF16)] * CORE_KV,
            jax.ShapeDtypeStruct((2 * nb, CORE_KV, 1, STACK), F32),
        ],
        compiler_params=params(1),
        cost_estimate=cost(weight),
        name="attention_forward",
    )(bl, bc, meta, q, *kvs)


def backward_kernel(nc, nb, plan, width, bl_ref, bc_ref, meta_ref, q_ref, a_ref, st_ref, *rest):
    kv_refs, rest = rest[:nc], rest[nc:]
    if plan:
        (g0_ref, g1_ref, *w_refs), (dq_ref, dkv_ref, spare_ref, kv_sc, acc, do_ref) = rest[:-6], rest[-6:]
    else:
        do_ref, dq_ref, dkv_ref, kv_sc, acc = rest
    i = pl.program_id(0)
    rows = nb * BLOCK_SIZE

    @pl.when(i == 0)
    def _():
        if plan:
            for span, part in output_grad_product(plan, width, meta_ref, (g0_ref, g1_ref), w_refs):
                spare_ref[:, span] = part[:rows].astype(BF16)
                do_ref[:, span] = part[rows:].astype(BF16)
        fill_kv(kv_refs, kv_sc, rows, nc)
        acc[...] = jnp.zeros_like(acc)

    c = meta_ref[0]
    count = bc_ref[i]

    def run(slots):
        starts = [slot_rows(bl_ref, c, i, j, nb) for j in range(slots)]
        here = pl.ds(pl.multiple_of(i * BLOCK_SIZE, BLOCK_SIZE), BLOCK_SIZE)
        for g in range(CORE_KV):
            qs = wide_part(q_ref, g)
            dos = stack_heads(do_ref[here, g * WIDE:(g + 1) * WIDE])
            outs = wide_part(a_ref, g)
            row_dot = jnp.sum((dos.astype(F32) * outs.astype(F32)).T, axis=0, keepdims=True)
            k_cat = slot_cat(kv_sc, 0, g, starts)
            v_cat = slot_cat(kv_sc, 0, CORE_KV + g, starts)
            s_t = masked_scores(k_cat, qs, slots, count)
            p = jnp.exp2(s_t * EXP2_SCALE - st_ref[0, g])
            dp = lax.dot_general(v_cat, dos, NT, preferred_element_type=F32)
            ds = (p * (dp - row_dot)).astype(BF16)
            dv = dot(p.astype(BF16), dos)
            dk = dot(ds, qs) * SCALE
            dq_t = lax.dot_general(k_cat, ds, TN, preferred_element_type=F32) * SCALE
            for h in range(GROUP):
                part = dq_t[:, h * BLOCK_SIZE:(h + 1) * BLOCK_SIZE]
                lane = g * WIDE + h * HEAD_DIM
                dq_ref[:, lane:lane + HEAD_DIM] = part.astype(BF16).T
            lanes = slice(g * HEAD_DIM, (g + 1) * HEAD_DIM)
            for j in range(slots):
                at = pl.ds(pl.multiple_of(bl_ref[i, j] * BLOCK_SIZE, BLOCK_SIZE), BLOCK_SIZE)
                acc[0, at, lanes] += dk[j * BLOCK_SIZE:(j + 1) * BLOCK_SIZE]
                acc[1, at, lanes] += dv[j * BLOCK_SIZE:(j + 1) * BLOCK_SIZE]

    by_count(count, run)

    @pl.when(i == nb - 1)
    def _():
        dkv_ref[...] = acc[...].astype(BF16)


def backward(bl, bc, meta, s, q, a, st, kvs, extra, plan=(), weight=20):
    nc, rows = len(kvs), q.shape[1]
    nb, width = rows // BLOCK_SIZE, extra[-1].shape[-1]
    wide = pl.BlockSpec((1, BLOCK_SIZE, HALF), lambda n, *_: (s, n, 0))
    whole = pl.BlockSpec(memory_space=pltpu.VMEM)
    grad = jax.ShapeDtypeStruct((rows, HALF), BF16)
    return pl.pallas_call(
        functools.partial(backward_kernel, nc, nb, plan, width),
        grid_spec=pltpu.PrefetchScalarGridSpec(
            num_scalar_prefetch=3,
            grid=(nb,),
            in_specs=[
                wide,
                wide,
                pl.BlockSpec((1, CORE_KV, 1, STACK), lambda n, *_: (s * nb + n, 0, 0, 0)),
                *[whole] * (nc + len(extra)),
            ],
            out_specs=[
                pl.BlockSpec((BLOCK_SIZE, HALF), lambda n, *_: (n, 0)),
                pl.BlockSpec((2, nc * rows, KV_HALF), lambda n, *_: (0, 0, 0)),
                *[pl.BlockSpec((rows, HALF), lambda n, *_: (0, 0))] * bool(plan),
            ],
            scratch_shapes=[
                pltpu.VMEM((1, 2 * CORE_KV, nc * rows, HEAD_DIM), BF16),
                pltpu.VMEM((2, nc * rows, KV_HALF), F32),
                *[pltpu.VMEM((rows, HALF), BF16)] * bool(plan),
            ],
        ),
        out_shape=[grad, jax.ShapeDtypeStruct((2, nc * rows, KV_HALF), BF16), *[grad] * bool(plan)],
        compiler_params=params(1),
        cost_estimate=cost(weight),
        name="attention_backward",
    )(bl, bc, meta, q, a, st, *kvs, *extra)


def column(meta_ref, chip, core, width):
    at = ((meta_ref[2] ^ chip) * 2 + (meta_ref[1] ^ core)) * width
    return pl.ds(pl.multiple_of(at, width), width)


def read_piece(w_refs, piece):
    ref, lead, start = piece
    rows = pl.ds(start, HALF // 2)
    return w_refs[ref][rows, :] if lead is None else w_refs[ref][lead, rows, :]


def output_grad_product(plan, width, meta_ref, g_refs, w_refs):
    grads = jnp.concatenate(
        [
            jnp.concatenate([ref[:, column(meta_ref, chip, core, width)] for ref in g_refs], axis=0)
            for chip, core, _ in plan
        ],
        axis=1,
    )
    for r in range(2):
        w = jnp.concatenate([read_piece(w_refs, pieces[r]) for _, _, pieces in plan], axis=1)
        yield slice(r * (HALF // 2), (r + 1) * (HALF // 2)), lax.dot_general(
            grads, w, NT, preferred_element_type=F32
        )


def mix_kernel(plan, width, meta_ref, a_ref, resid_ref, *rest):
    w_refs, (own_ref, other_ref) = rest[:-2], rest[-2:]
    rows = resid_ref.shape[0]
    a = jnp.concatenate([a_ref[0], a_ref[1]], axis=0)
    for chip, core, pieces in plan:
        at = column(meta_ref, chip, core, width)
        part = dot(a, jnp.concatenate([read_piece(w_refs, piece) for piece in pieces], axis=0))
        own_ref[:, at] = part[:rows] + resid_ref[:, at].astype(F32)
        other_ref[:, at] = part[rows:].astype(BF16)


def mix(meta, a, resid, plan, arrays, weight=20):
    width = arrays[0].shape[-1]
    whole = pl.BlockSpec(memory_space=pltpu.VMEM)
    return pl.pallas_call(
        functools.partial(mix_kernel, plan, width),
        in_specs=[pl.BlockSpec(memory_space=pltpu.SMEM)] + [whole] * (2 + len(arrays)),
        out_specs=[whole, whole],
        out_shape=[jax.ShapeDtypeStruct(resid.shape, F32), jax.ShapeDtypeStruct(resid.shape, BF16)],
        compiler_params=params(0),
        cost_estimate=cost(weight),
        name="mix",
    )(meta, a, resid, *arrays)


def proj_kernel(count, width, cols_ref, g0_ref, g1_ref, *refs):
    inputs, outputs = refs[:8], refs[8:]
    for r in range(2):
        at_ref, far_ref, near0_ref, near1_ref = inputs[4 * r:4 * r + 4]
        lhs = jnp.concatenate([at_ref[0], at_ref[1], far_ref[0], far_ref[1]], axis=1)
        for n in range(count):
            for side in range(2):
                own = pl.ds(pl.multiple_of(cols_ref[r, n, side, 0], width), width)
                near = pl.ds(pl.multiple_of(cols_ref[r, n, side, 1], width), width)
                rhs = [g0_ref[:, own], g1_ref[:, own], near0_ref[:, near], near1_ref[:, near]]
                out = dot(lhs, jnp.concatenate(rhs, axis=0))
                outputs[(r * count + n) * 2 + side][...] = out.astype(BF16)


def proj_parts(cols, g0, g1, inputs, width, weight=20):
    count = cols.shape[1]
    whole = pl.BlockSpec(memory_space=pltpu.VMEM)
    return pl.pallas_call(
        functools.partial(proj_kernel, count, width),
        in_specs=[pl.BlockSpec(memory_space=pltpu.SMEM)] + [whole] * 10,
        out_specs=[whole] * (4 * count),
        out_shape=[jax.ShapeDtypeStruct((WIDE, width), BF16)] * (4 * count),
        compiler_params=params(0),
        cost_estimate=cost(weight),
        name="proj_parts",
    )(cols, g0, g1, *inputs)


def halve_kernel(meta_ref, q0_ref, q1_ref, out_ref):
    out_ref[0] = q0_ref[...]
    out_ref[1] = q1_ref[...]


def halve(meta, q0, q1, weight=20):
    rows = q0.shape[0]
    half = pl.BlockSpec((rows, HALF), lambda n, m: (0, m[1]))
    return pl.pallas_call(
        halve_kernel,
        grid_spec=pltpu.PrefetchScalarGridSpec(
            num_scalar_prefetch=1,
            grid=(1,),
            in_specs=[half, half],
            out_specs=pl.BlockSpec((2, rows, HALF), lambda n, m: (0, 0, 0)),
        ),
        out_shape=jax.ShapeDtypeStruct((2, rows, HALF), BF16),
        compiler_params=params(1),
        cost_estimate=cost(weight),
        name="halve",
    )(meta, q0, q1)


def after(x, *earlier):
    return lax.optimization_barrier((x, *earlier))[0]


def local(nc, nf, queries, keys, values, resid, grad_out, w_out, block_list, block_count):
    chips = nf // 2
    bits = [1 << b for b in range(chips.bit_length() - 1)]
    routes = (bits, bits[::-1])
    mid = HALF // 2
    c = lax.axis_index("ctx")
    f = lax.axis_index("fsdp")
    core, chip = f % 2, f // 2
    meta = jnp.stack([c, core, chip]).astype(jnp.int32)
    rows = queries.shape[1]
    width = w_out.shape[1]

    def to_core(x):
        return lax.ppermute(x, "fsdp", [(p, p ^ 1) for p in range(nf)])

    def to_chip(x, bit):
        return lax.ppermute(x, "fsdp", [(p, p ^ (2 * bit)) for p in range(nf)])

    def place(mine, theirs, axis):
        return jnp.where(
            core == 0,
            jnp.concatenate([mine, theirs], axis=axis),
            jnp.concatenate([theirs, mine], axis=axis),
        )

    def kv_part(which):
        cut = lambda x: lax.dynamic_slice_in_dim(x[0], which * KV_HALF, KV_HALF, 1)
        return jnp.concatenate([cut(keys), cut(values)], axis=1)

    def hop_up(x, step):
        return lax.ppermute(x, "ctx", [(p, p + 1) for p in range(step - 1, nc - 1)])

    q0, g0 = queries[0], grad_out[0]
    w_mine = lax.dynamic_slice_in_dim(w_out, core * HALF, HALF, 0)
    kvs0 = [kv_part(core)]
    kvs1 = [to_core(kv_part(1 - core))]
    w_theirs = to_core(lax.dynamic_slice_in_dim(w_out, (1 - core) * HALF, HALF, 0))

    arrays = [w_mine, w_theirs]
    held = {(0, side, r): (side, None, r * mid) for side in range(2) for r in range(2)}
    last = {}
    for side in range(2):
        for bit in bits:
            got = to_chip(after(arrays[side], *last.get(bit, ())), bit)
            for r in range(2):
                held[bit, side, r] = (len(arrays), None, r * mid)
            arrays.append(got)
            last[bit] = (got,)
    for step in range(1, nc):
        kvs0.append(hop_up(kvs0[-1], step))
        kvs1.append(hop_up(kvs1[-1], step))
    for step in range(1, len(bits)):
        for r in range(2):
            bit = routes[r][step]
            known = [0]
            for earlier in routes[r][:step]:
                known += [rel ^ earlier for rel in known]
            sources = [(rel, side) for rel in known[1:] for side in range(2)]
            parts = []
            for source in sources:
                ref, lead, first = held[(*source, r)]
                x = arrays[ref] if lead is None else arrays[ref][lead]
                parts.append(x[first:first + mid])
            got = to_chip(after(jnp.stack(parts), *last[bit], kvs0[nc - 2], kvs1[nc - 2]), bit)
            for n, (rel, side) in enumerate(sources):
                held[rel ^ bit, side, r] = (len(arrays), n, 0)
            arrays.append(got)
            last[bit] = (got,)
    w_gate = [x for bit in bits for x in last[bit]]
    g1 = to_core(after(g0, w_theirs, kvs1[0]))
    q1 = to_core(after(q0, g1))
    plan = [
        (rel, core_bit, [held[rel, core_bit, r] for r in range(2)]) for rel in range(chips) for core_bit in range(2)
    ]
    with_bit = [[rel for rel in range(chips) if rel & route[0]] for route in routes]
    without = [[rel ^ routes[r][0] for rel in with_bit[r]] for r in range(2)]

    def grad_columns(rels):
        cut = lambda rel: lax.dynamic_slice_in_dim(g0, (chip ^ rel) * 2 * width, 2 * width, 1)
        return jnp.concatenate([cut(rel) for rel in rels], axis=1)

    q_both = halve(meta, after(q0, kvs0[nc - 2], kvs1[nc - 2]), q1)
    kvs0[-1], kvs1[-1] = after(kvs0[-1], q_both), after(kvs1[-1], q_both)
    kvs = kvs0 + kvs1
    a_both, *at, st = forward(block_list, block_count, meta, q_both, kvs)
    near_grads = []
    for r in range(2):
        got = to_chip(after(grad_columns(with_bit[r]), *w_gate, a_both), routes[r][0])
        near_grads.append((got, to_core(got)))
    far_at = [to_chip(after(at[r], near_grads[r][0]), routes[r][0]) for r in range(2)]
    def total(parts):
        return functools.reduce(jnp.add, [x.astype(F32) for x in parts])

    class Chain:
        def __init__(self, shard, sign):
            self.shard, self.sign, self.step = shard, sign, 0

        def send(self):
            self.step += 1
            t = jnp.clip(c - self.sign * (self.step - nc), 0, nc - 1)
            own = self.shard(t)
            self.sent = own if self.step == 1 else total([own, self.got]).astype(BF16)
            reach = [p for p in range(nc) if (nc - 1 - p if self.sign < 0 else p) < self.step]
            pairs = [(p, p + self.sign) for p in reach if 0 <= p + self.sign < nc]
            self.got = lax.ppermute(self.sent, "ctx", pairs)

        def gate(self, *earlier):
            self.got = after(self.got, *earlier)

        def result(self):
            while self.step < nc - 1:
                self.send()
            return self.got

    kv_shard = lambda dkv: lambda t: lax.dynamic_slice_in_dim(dkv, t * rows, rows, 1)
    listed = (block_list, block_count, meta)
    dq1, dkv1, do0 = backward(*listed, 1, q_both, a_both, st, kvs1, (g0, g1, *arrays), plan)

    def hop_down(step, got):
        parts = []
        for lane, dkv in ((0, dkv1), (1, dkv0)):
            hop = step - lane
            if 1 <= hop < nc:
                own = kv_shard(dkv)(jnp.maximum(c + hop - nc, 0))
                parts.append(own if hop == 1 else total([own, got[lane]]).astype(BF16))
            else:
                parts.append(None)
        sending = jnp.stack([x for x in parts if x is not None])
        moved = lax.ppermute(sending, "ctx", [(p, p - 1) for p in range(max(nc - step, 1), nc)])
        return sending, moved

    def unpack(step, moved):
        return (moved[0] if step < nc else None, moved[-1] if step > 1 else None)

    dkv0 = None
    sending, moved = hop_down(1, None)
    dq0, dkv0 = backward(*listed, 0, after(q_both, sending), a_both, st, kvs0, (do0,))
    sending, moved = hop_down(2, unpack(1, after(moved, dkv0)))

    inputs = []
    for r in range(2):
        inputs += [at[r], after(far_at[r], dkv0), *near_grads[r]]
    order = [
        [[jnp.stack([((chip ^ rel) * 2 + (core ^ side)) * width, (n * 2 + (core ^ side)) * width]) for side in range(2)]
         for n, rel in enumerate(without[r])]
        for r in range(2)
    ]
    cols = jnp.stack([jnp.stack([jnp.stack(pair) for pair in route]) for route in order]).astype(jnp.int32)
    parts = proj_parts(after(cols, sending), g0, g1, inputs, width)
    count = len(without[0])
    own_mix, other_mix = mix(meta, after(a_both, parts[0]), resid[0], plan, arrays)
    sending, moved = hop_down(3, unpack(2, after(moved, other_mix)))
    for step in range(4, nc + 1):
        if step == nc:
            sum1 = total([kv_shard(dkv1)(c), moved[0]]).astype(BF16)
        sending_more, moved = hop_down(step, unpack(step - 1, moved))
    sum0 = total([kv_shard(dkv0)(c), moved[-1]]).astype(BF16)
    query_grad = place(dq0, to_core(after(dq1, other_mix)), 1)[None]

    def reduce_chips(r):
        have = {(rel, side): parts[(r * count + n) * 2 + side] for n, rel in enumerate(without[r]) for side in range(2)}
        for bit in routes[r][1:-1]:
            far = sorted({rel for rel, _ in have if rel & bit})
            for side in range(2):
                got = to_chip(jnp.stack([have.pop((rel, side)).astype(BF16) for rel in far]), bit)
                for n, rel in enumerate(far):
                    have[rel ^ bit, side] = total([have[rel ^ bit, side], got[n]])
        bit = routes[r][-1]
        same = to_chip(have[bit, 0].astype(BF16), bit)
        cross = lax.ppermute(have[bit, 1].astype(BF16), "fsdp", [(p, p ^ (2 * bit) ^ 1) for p in range(nf)])
        return have[0, 0], have[0, 1], after(same, other_mix), after(cross, other_mix)

    reduced = [reduce_chips(r) for r in range(2)]
    swapped = to_core(after(jnp.concatenate([part[1].astype(BF16) for part in reduced], axis=0), other_mix))
    mine = [total([near, same]) for near, _, same, _ in reduced]
    theirs = [total([swapped[r * mid:(r + 1) * mid], reduced[r][3]]) for r in range(2)]
    proj_rows = jnp.concatenate(mine + theirs, axis=0).astype(BF16)
    proj_rows = after(proj_rows, sending)
    share = QUERY_HEADS * HEAD_DIM // nc

    def proj_shard(t):
        start = t * share
        return lax.dynamic_slice_in_dim(proj_rows, start + (core * HALF) * jnp.where(start < HALF, 1, -1), share, 0)

    proj_down, proj_up = Chain(proj_shard, -1), Chain(proj_shard, 1)
    for _ in range(nc - 1):
        proj_down.send()
        proj_up.send()
        proj_down.got, proj_up.got = lax.optimization_barrier((proj_down.got, proj_up.got))
    proj_grad = total([proj_shard(c), proj_down.got, proj_up.got])
    mixed = total([own_mix, to_core(other_mix)]).astype(BF16)
    grads = place(sum0, to_core(sum1), 2)
    return mixed[None], query_grad, grads[:1], grads[1:], proj_grad


def solution(mesh):
    rows = P("fsdp", "ctx", None)
    body = functools.partial(local, mesh.shape["ctx"], mesh.shape["fsdp"])
    return jax.shard_map(
        body,
        mesh=mesh,
        in_specs=(rows, rows, rows, rows, rows, P(None, "fsdp"), P("ctx", None), P("ctx")),
        out_specs=(rows, rows, rows, rows, P("ctx", "fsdp")),
        check_vma=False,
    )
```
